32 devices in a mesh: ctx: 8 (over z, y), tp: 4 (over x, core).
Axes of the slice: x: 2, y: 2, z: 4, core: 2. Of those that a mesh axis runs over, the one named last changes fastest.
Arguments:
- lin_query: bfloat16 [2048, 4096], P('ctx', 'tp'), may hold values from -6 to 6
- lin_key: bfloat16 [2048, 4096], P('ctx', 'tp'), may hold values from -0.35 to 0.35
- lin_value: bfloat16 [2048, 4096], P('ctx', 'tp'), may hold values from -7 to 7
- log_decay: float32 [32, 2048], P('tp', 'ctx'), may hold values from -1 to 0
- norm_gain: float32 [4096], P('tp'), may hold values from 0.5 to 1.5
- lin_gate: bfloat16 [2048, 4096], P('ctx', 'tp'), may hold values from -6 to 6
- lin_grad: bfloat16 [2048, 4096], P('ctx', 'tp'), may hold values from -6 to 6
- soft_query: bfloat16 [2048, 4096], P('ctx', 'tp'), may hold values from -6 to 6
- soft_key: bfloat16 [2048, 1024], P('ctx', 'tp'), may hold values from -6 to 6
- soft_value: bfloat16 [2048, 1024], P('ctx', 'tp'), may hold values from -6 to 6
- soft_grad: bfloat16 [2048, 4096], P('ctx', 'tp'), may hold values from -6 to 6
Outputs:
- lin_out: bfloat16 [2048, 4096], P('ctx', 'tp')
- lin_query_grad: bfloat16 [2048, 4096], P('ctx', 'tp')
- lin_key_grad: bfloat16 [2048, 4096], P('ctx', 'tp')
- lin_value_grad: bfloat16 [2048, 4096], P('ctx', 'tp')
- lin_gate_grad: bfloat16 [2048, 4096], P('ctx', 'tp')
- soft_out: bfloat16 [2048, 4096], P('ctx', 'tp')
- soft_query_grad: bfloat16 [2048, 4096], P('ctx', 'tp')
- soft_key_grad: bfloat16 [2048, 1024], P('ctx', 'tp')
- soft_value_grad: bfloat16 [2048, 1024], P('ctx', 'tp')
The draws below stay inside these ranges and needn't reach their ends.
All inputs are finite; a program needn't handle non-finite values.
Results may differ from the reference program's by a relative error of at most 0.035.
Values may be sent and summed in bfloat16 or wider, within the bound.
No kernel may reach another device: no remote copies, remote signals or barrier semaphores. Data moves between devices by JAX's collectives and lax.ppermute only.
A program may use at most 128 MiB of HBM per device.

```python
import math
import jax
import jax.numpy as jnp
from jax import lax

DH = 128
LINEAR_HEADS = 32
QS = 32
KVS = 8
TOK_DEV = 256
TOKEN_COUNT = 2048
N_CTX = 8


def head_classes(key, fast_share, medium_share):
    pick = jax.random.uniform(jax.random.fold_in(key, 41), (LINEAR_HEADS,), jnp.float32, 0.0, 1.0)
    fast_heads = pick < fast_share
    medium_heads = (pick >= fast_share) & (pick < fast_share + medium_share)
    phase = jax.random.randint(jax.random.fold_in(key, 43), (LINEAR_HEADS,), 0, 8)
    return (fast_heads, medium_heads, phase)


def draw_lin_key(key, part):
    width = LINEAR_HEADS * DH
    fast_share = 0.25
    medium_share = 0.25
    base = jax.random.normal(jax.random.fold_in(key, 4), (TOKEN_COUNT, width), jnp.float32) * DH ** (-0.5)
    base = jnp.clip(base, -0.35, 0.35)
    fast_heads, medium_heads, phase = head_classes(key, fast_share, medium_share)
    block_ids = jnp.arange(TOKEN_COUNT) // TOK_DEV
    loud_blocks = (block_ids[:, None] + phase[None, :]) % 8 == 0
    head_level = jnp.where(medium_heads[None, :], jnp.where(loud_blocks, 1.0, 0.02), 0.1)
    level = jnp.repeat(head_level, DH, axis=1)
    return (base * level).astype(jnp.bfloat16)


def draw_lin_value(key, part):
    width = LINEAR_HEADS * DH
    fraction = jnp.arange(width, dtype=jnp.float32) / (width - 1)
    base = jnp.clip(jax.random.normal(jax.random.fold_in(key, 3), (TOKEN_COUNT, width), jnp.float32), -4.0, 4.0)
    column_scale = jnp.exp(fraction * 0.5 * math.log(3.0))
    return (base * column_scale[None, :]).astype(jnp.bfloat16)


def draw_log_decay(key, part):
    random_root_key = jax.random.fold_in(key, 5)
    medium_random_key, gradual_random_key, machine_random_key, spike_random_key, position_random_key, noise_random_key = jax.random.split(random_root_key, 6)
    fast_share = 0.25
    medium_share = 0.25
    fast_heads, medium_heads, phase = head_classes(key, fast_share, medium_share)
    fast_rate = jnp.exp(jax.random.uniform(noise_random_key, (LINEAR_HEADS, 1), jnp.float32, math.log(0.012), math.log(0.02)))
    medium_rate = 0.5 / TOK_DEV * jnp.exp(jax.random.uniform(medium_random_key, (LINEAR_HEADS, 1), jnp.float32, 0.0, math.log(1.4)))
    slow_rate = 0.2 / TOKEN_COUNT * jnp.exp(jax.random.uniform(gradual_random_key, (LINEAR_HEADS, 1), jnp.float32, 0.0, math.log(2.0)))
    head_decay_rate = jnp.where(fast_heads[:, None], fast_rate, jnp.where(medium_heads[:, None], medium_rate, slow_rate))
    machine_factor = jnp.exp(jax.random.uniform(machine_random_key, (LINEAR_HEADS, TOKEN_COUNT // TOK_DEV), jnp.float32, 0.0, math.log(2.0)))
    machine_factor = jnp.repeat(machine_factor, TOK_DEV, axis=1)
    places = jax.random.randint(position_random_key, (2,), 0, TOKEN_COUNT)
    struck_rows = jnp.any(jnp.arange(TOKEN_COUNT)[None, :] == places[:, None], axis=0)
    spike_depth = jnp.log(jax.random.uniform(spike_random_key, (LINEAR_HEADS, TOKEN_COUNT), jnp.float32, 0.5, 0.8))
    return -head_decay_rate * machine_factor + jnp.where(struck_rows[None, :], spike_depth, 0.0)


def draw_soft_query(key, part):
    width = QS * DH
    base = jnp.clip(2.0 * jax.random.normal(jax.random.fold_in(key, 1), (TOKEN_COUNT, width), jnp.float32), -6.0, 6.0)
    return base.astype(jnp.bfloat16)


def draw_soft_key(key, part):
    width = KVS * DH
    base = jnp.clip(jax.random.normal(jax.random.fold_in(key, 2), (TOKEN_COUNT, width), jnp.float32), -4.0, 4.0)
    loud_rows = TOKEN_COUNT - 1 - jax.random.randint(jax.random.fold_in(key, 7), (KVS,), 0, 8)
    loud_signs = jnp.where(jax.random.bernoulli(jax.random.fold_in(key, 9), 0.5, (width,)), 6.0, -6.0)
    column_head = jnp.arange(width) // DH
    column_row = jnp.sum(jnp.where(column_head[:, None] == jnp.arange(KVS)[None, :], loud_rows[None, :], 0), axis=1)
    struck = jnp.arange(TOKEN_COUNT)[:, None] == column_row[None, :]
    base = jnp.where(struck, loud_signs[None, :], base)
    return base.astype(jnp.bfloat16)


def level_of(stream_key, shape, shards, least, largest):
    gain = 1.0
    for axis_at, shards_of in shards:
        draws = jax.random.uniform(jax.random.fold_in(jax.random.fold_in(stream_key, 6), axis_at), (shards_of,), jnp.float32, least / len(shards), largest / len(shards))
        gain = gain * jnp.repeat(jnp.exp(draws), shape[axis_at] // shards_of).reshape((-1,) + (1,) * (len(shape) - 1 - axis_at))
    return gain


def noise(own_key, extent, scale, bound, cuts=(), kind=jnp.bfloat16):
    drawn = scale * jax.random.normal(own_key, extent, jnp.float32)
    if cuts:
        drawn = drawn * level_of(own_key, extent, cuts, -0.22, 0.18)
    return jnp.clip(drawn, -bound, bound).astype(kind)


def setup_inputs(seed: int = 0) -> dict:
    key_list = jax.random.split(jax.random.key(seed), 12)
    lin_query = noise(key_list[0], (TOKEN_COUNT, LINEAR_HEADS * DH), 1.0, 6.0, ((0, 8), (1, 4)))
    lin_key = draw_lin_key(jax.random.fold_in(key_list[11], 71), 0)
    lin_value = draw_lin_value(jax.random.fold_in(key_list[11], 71), 0)
    log_decay = draw_log_decay(jax.random.fold_in(key_list[11], 71), 0)
    norm_gain = jnp.clip(1.0 + 0.1 * jax.random.normal(key_list[4], (LINEAR_HEADS * DH,), jnp.float32), 0.5, 1.5)
    lin_gate = noise(key_list[5], (TOKEN_COUNT, LINEAR_HEADS * DH), 1.0, 6.0, ((0, 8), (1, 4)))
    lin_grad = noise(key_list[6], (TOKEN_COUNT, LINEAR_HEADS * DH), 1.0, 6.0, ((0, 8), (1, 4)))
    soft_query = draw_soft_query(jax.random.fold_in(key_list[11], 71), 0)
    soft_key = draw_soft_key(jax.random.fold_in(key_list[11], 71), 0)
    soft_value = noise(key_list[9], (TOKEN_COUNT, KVS * DH), 1.0, 6.0, ((0, 8), (1, 4)))
    soft_grad = noise(key_list[10], (TOKEN_COUNT, QS * DH), 1.0, 6.0, ((0, 8), (1, 4)))
    return dict(lin_query=lin_query, lin_key=lin_key, lin_value=lin_value, log_decay=log_decay, norm_gain=norm_gain, lin_gate=lin_gate, lin_grad=lin_grad, soft_query=soft_query, soft_key=soft_key, soft_value=soft_value, soft_grad=soft_grad)


top_precision = lax.Precision.HIGHEST

def round_bf16(values):
    return lax.optimization_barrier(values.astype(jnp.bfloat16)).astype(jnp.float32)

def block_parts(log_block):
    blocklog = jnp.cumsum(log_block, axis=1)
    totals = blocklog[:, -1]
    order_ids = jnp.arange(log_block.shape[1])
    causal = (order_ids[:, None] >= order_ids[None, :])[None]
    spread = blocklog[:, :, None] - blocklog[:, None, :]
    decay_mask = jnp.where(causal, jnp.exp(jnp.where(causal, spread, 0.0)), 0.0)
    tail_decay = jnp.exp(totals[:, None] - blocklog).T[:, :, None]
    lead_decay = jnp.exp(blocklog).T[:, :, None]
    return (decay_mask, tail_decay, lead_decay, totals)

def lightning_reference(lin_query, lin_key, lin_value, log_decay, norm_gain, lin_gate, lin_grad):
    width = LINEAR_HEADS * DH
    shape_four = (N_CTX, TOK_DEV, LINEAR_HEADS, DH)
    query_blocks = lin_query.reshape(shape_four)
    key_blocks = lin_key.reshape(shape_four)
    value_blocks = lin_value.reshape(shape_four)
    log_blocks = log_decay.reshape(LINEAR_HEADS, N_CTX, TOK_DEV).transpose(1, 0, 2)

    def forward_step(chain_state, block_data):
        query_block, key_block, value_block, log_block = block_data
        decay_mask, tail_decay, lead_decay, totals = block_parts(log_block)
        query_f = query_block.astype(jnp.float32)
        key_f = key_block.astype(jnp.float32)
        value_f = value_block.astype(jnp.float32)
        raw_scores = jnp.einsum('thd,shd->hts', query_f, key_f, precision=top_precision)
        weights = round_bf16(raw_scores * decay_mask)
        attended = jnp.einsum('hts,she->the', weights, value_f, precision=top_precision)
        attended = attended + jnp.einsum('thd,hde->the', query_f * lead_decay, chain_state, precision=top_precision)
        local_state = jnp.einsum('shd,she->hde', key_f * tail_decay, value_f, precision=top_precision)
        following = jnp.exp(totals)[:, None, None] * chain_state + local_state
        return (following, (attended, chain_state))
    initial = jnp.zeros((LINEAR_HEADS, DH, DH), jnp.float32)
    _, (attended, carried) = lax.scan(forward_step, initial, (query_blocks, key_blocks, value_blocks, log_blocks))
    flat_out = attended.reshape(TOKEN_COUNT, width)
    scaling = lax.rsqrt(lax.optimization_barrier(jnp.sum(flat_out * flat_out, axis=1)) / width + 1e-05)[:, None]
    normed = flat_out * scaling
    gate_sig = jax.nn.sigmoid(lin_gate.astype(jnp.float32))
    gain_row = norm_gain[None, :]
    lin_out = (normed * gain_row * gate_sig).astype(jnp.bfloat16)
    grad_f = lin_grad.astype(jnp.float32)
    scaled = grad_f * gain_row * gate_sig
    gate_grad = (grad_f * normed * gain_row * gate_sig * (1.0 - gate_sig)).astype(jnp.bfloat16)
    cross_term = lax.optimization_barrier(jnp.sum(scaled * normed, axis=1)) / width
    att_grad = scaling * (scaled - normed * cross_term[:, None])
    grad_blocks = att_grad.astype(jnp.bfloat16).reshape(shape_four)

    def backward_step(chain_grad, block_data):
        query_block, key_block, value_block, log_block, grad_block, chain_state = block_data
        decay_mask, tail_decay, lead_decay, totals = block_parts(log_block)
        query_f = query_block.astype(jnp.float32)
        key_f = key_block.astype(jnp.float32)
        value_f = value_block.astype(jnp.float32)
        grad_blk = grad_block.astype(jnp.float32)
        raw_scores = jnp.einsum('thd,shd->hts', query_f, key_f, precision=top_precision)
        weights = round_bf16(raw_scores * decay_mask)
        grad_raw = jnp.einsum('the,she->hts', grad_blk, value_f, precision=top_precision)
        grad_weights = round_bf16(grad_raw * decay_mask)
        query_grad = jnp.einsum('hts,shd->thd', grad_weights, key_f, precision=top_precision)
        query_grad = query_grad + jnp.einsum('the,hde->thd', grad_blk * lead_decay, chain_state, precision=top_precision)
        key_grad = jnp.einsum('hts,thd->shd', grad_weights, query_f, precision=top_precision)
        key_grad = key_grad + jnp.einsum('she,hde->shd', value_f * tail_decay, chain_grad, precision=top_precision)
        value_grad = jnp.einsum('hts,the->she', weights, grad_blk, precision=top_precision)
        value_grad = value_grad + jnp.einsum('shd,hde->she', key_f * tail_decay, chain_grad, precision=top_precision)
        local_grad = jnp.einsum('thd,the->hde', query_f * lead_decay, grad_blk, precision=top_precision)
        following = jnp.exp(totals)[:, None, None] * chain_grad + local_grad
        return (following, (query_grad, key_grad, value_grad))
    _, (query_grad, key_grad, value_grad) = lax.scan(backward_step, initial, (query_blocks, key_blocks, value_blocks, log_blocks, grad_blocks, carried), reverse=True)
    return (lin_out, query_grad.reshape(TOKEN_COUNT, width).astype(jnp.bfloat16), key_grad.reshape(TOKEN_COUNT, width).astype(jnp.bfloat16), value_grad.reshape(TOKEN_COUNT, width).astype(jnp.bfloat16), gate_grad)

def soft_reference(soft_query, soft_key, soft_value, soft_grad):
    group_size = QS // KVS
    score_scale = DH ** (-0.5)
    query_heads = soft_query.reshape(TOKEN_COUNT, KVS, group_size, DH).transpose(1, 0, 2, 3)
    grad_heads = soft_grad.reshape(TOKEN_COUNT, KVS, group_size, DH).transpose(1, 0, 2, 3)
    key_heads = soft_key.reshape(TOKEN_COUNT, KVS, DH).transpose(1, 0, 2)
    value_heads = soft_value.reshape(TOKEN_COUNT, KVS, DH).transpose(1, 0, 2)
    block_rows = min(512, TOKEN_COUNT)
    block_count = TOKEN_COUNT // block_rows
    key_ids = jnp.arange(TOKEN_COUNT)

    def per_head(head_data):
        query_head, grad_head, key_head, value_head = head_data
        key_f = key_head.astype(jnp.float32)
        value_f = value_head.astype(jnp.float32)

        def block_step(running, block_index):
            start_row = (block_index * block_rows).astype(jnp.int32)
            query_f = lax.dynamic_slice_in_dim(query_head, start_row, block_rows, 0).astype(jnp.float32)
            grad_f = lax.dynamic_slice_in_dim(grad_head, start_row, block_rows, 0).astype(jnp.float32)
            positions = start_row + jnp.arange(block_rows)
            allowed = (positions[:, None] >= key_ids[None, :])[None]
            scores = jnp.einsum('rgd,cd->grc', query_f, key_f, precision=top_precision) * score_scale
            row_peak = lax.optimization_barrier(jnp.max(jnp.where(allowed, scores, -jnp.inf), axis=-1))
            raw_probs = jnp.where(allowed, jnp.exp(scores - row_peak[..., None]), 0.0)
            row_total = lax.optimization_barrier(jnp.sum(raw_probs, axis=-1))
            weights = round_bf16(raw_probs)
            out_f = jnp.einsum('grc,cd->grd', weights, value_f, precision=top_precision) / row_total[..., None]
            out_block = out_f.transpose(1, 0, 2).astype(jnp.bfloat16)
            out_back = lax.optimization_barrier(out_block).astype(jnp.float32)
            logsum = row_peak + jnp.log(row_total)
            delta_rows = lax.optimization_barrier(jnp.sum(grad_f * out_back, axis=-1)).T
            probs = jnp.where(allowed, jnp.exp(scores - logsum[..., None]), 0.0)
            prob_grad = jnp.einsum('rgd,cd->grc', grad_f, value_f, precision=top_precision)
            score_grad = round_bf16(probs * (prob_grad - delta_rows[..., None]))
            query_grad = (jnp.einsum('grc,cd->rgd', score_grad, key_f, precision=top_precision) * score_scale).astype(jnp.bfloat16)
            key_acc = running[0] + jnp.einsum('grc,rgd->cd', score_grad, query_f, precision=top_precision) * score_scale
            value_acc = running[1] + jnp.einsum('grc,rgd->cd', round_bf16(probs), grad_f, precision=top_precision)
            return ((key_acc, value_acc), (out_block, query_grad))
        zero_rows = jnp.zeros((TOKEN_COUNT, DH), jnp.float32)
        (key_acc, value_acc), (outs, query_grads) = lax.scan(block_step, (zero_rows, zero_rows), jnp.arange(block_count))
        return (outs.reshape(TOKEN_COUNT, group_size, DH), query_grads.reshape(TOKEN_COUNT, group_size, DH), key_acc.astype(jnp.bfloat16), value_acc.astype(jnp.bfloat16))
    outs, query_grads, key_grads, value_grads = lax.map(per_head, (query_heads, grad_heads, key_heads, value_heads))
    soft_out = outs.transpose(1, 0, 2, 3).reshape(TOKEN_COUNT, QS * DH)
    query_grad = query_grads.transpose(1, 0, 2, 3).reshape(TOKEN_COUNT, QS * DH)
    key_grad = key_grads.transpose(1, 0, 2).reshape(TOKEN_COUNT, KVS * DH)
    value_grad = value_grads.transpose(1, 0, 2).reshape(TOKEN_COUNT, KVS * DH)
    return (soft_out, query_grad, key_grad, value_grad)

def reference(lin_query, lin_key, lin_value, log_decay, norm_gain, lin_gate, lin_grad, soft_query, soft_key, soft_value, soft_grad):
    lin_out, lin_query_grad, lin_key_grad, lin_value_grad, lin_gate_grad = lightning_reference(lin_query, lin_key, lin_value, log_decay, norm_gain, lin_gate, lin_grad)
    soft_out, soft_query_grad, soft_key_grad, soft_value_grad = soft_reference(soft_query, soft_key, soft_value, soft_grad)
    return (lin_out, lin_query_grad, lin_key_grad, lin_value_grad, lin_gate_grad, soft_out, soft_query_grad, soft_key_grad, soft_value_grad)
```

```python
import functools

import jax
import jax.numpy as jnp
from jax import lax
from jax.experimental import pallas as pl
from jax.experimental.pallas import tpu as pltpu
from jax.sharding import PartitionSpec as P

DH = 128
LOG2E = 1.4426950408889634
LN2 = 0.6931471805599453
negative_fill = -1e30
f32 = jnp.float32
bf16 = jnp.bfloat16
VMEM_BYTES = 48 * 1024 * 1024
CHUNK = 256

SMEM_SPEC = pl.BlockSpec(memory_space=pltpu.SMEM)
VMEM_SPEC = pl.BlockSpec(memory_space=pltpu.VMEM)


def nn(a, b):
    return jnp.dot(a, b, preferred_element_type=f32)


def nt(a, b):
    return lax.dot_general(a, b, (((1,), (1,)), ((), ())), preferred_element_type=f32)


def tn(a, b):
    return lax.dot_general(a, b, (((0,), (0,)), ((), ())), preferred_element_type=f32)


def whole_call(kernel, place, arrays, outs, flops=0):
    moved = sum(a.size * a.dtype.itemsize for a in arrays)
    moved += sum(int(jnp.dtype(o.dtype).itemsize) * o.size for o in outs)
    return pl.pallas_call(
        kernel,
        out_shape=outs,
        in_specs=[SMEM_SPEC] + [VMEM_SPEC] * len(arrays),
        out_specs=[VMEM_SPEC] * len(outs),
        compiler_params=pltpu.CompilerParams(vmem_limit_bytes=VMEM_BYTES),
        cost_estimate=pl.CostEstimate(flops=flops, bytes_accessed=moved, transcendentals=0),
    )(place, *arrays)


def split3(x):
    hi = x.astype(bf16)
    rest = x - hi.astype(f32)
    lo = rest.astype(bf16)
    return hi, lo, (rest - lo.astype(f32)).astype(bf16)


def extra_rows(heads):
    return 16 * pl.cdiv(3 * heads, 16)


def pack_logs(rows):
    heads = rows.shape[0]
    pad = extra_rows(heads) - 3 * heads
    parts = [p.astype(f32) for p in split3(rows)]
    if pad:
        parts.append(jnp.zeros((pad, DH), f32))
    return jnp.concatenate(parts, axis=0).astype(bf16)


def read_logs(ref, heads):
    part = ref[heads * DH :, :].astype(f32)
    return part[:heads] + part[heads : 2 * heads] + part[2 * heads : 3 * heads]


def head_rows(h):
    return slice(h * DH, (h + 1) * DH)


def lin_state_kernel(heads, fold, place, log_ref, key_ref, value_ref, msg_ref, row_ref, col_ref):
    rows = key_ref.shape[0]
    y = place[0]
    later = lax.broadcasted_iota(jnp.int32, (rows, rows), 0)
    earlier = lax.broadcasted_iota(jnp.int32, (rows, rows), 1)
    tri = (earlier <= later).astype(f32)
    logs = log_ref[...]
    exact = lax.Precision.HIGHEST
    dims = (((1,), (1,)), ((), ()))
    by_row = lax.dot_general(logs, tri, dims, precision=exact, preferred_element_type=f32)
    by_col = lax.dot_general(tri, logs, dims, precision=exact, preferred_element_type=f32)
    row_ref[...] = by_row
    col_ref[...] = by_col
    totals = by_row[:, rows - 1 : rows]
    tail = jnp.exp(totals - by_row)
    group = heads // fold
    for g in range(fold):
        slot = lax.rem(g + y, fold) if fold > 1 else 0
        for i in range(group):
            h = g * group + i
            key_t = key_ref[:, head_rows(h)].astype(f32).T * tail[h : h + 1, :]
            state = nn(key_t.astype(bf16), value_ref[:, head_rows(h)])
            msg_ref[slot, head_rows(i), :] = state.astype(bf16)
        wide = jnp.broadcast_to(totals[g * group : (g + 1) * group], (group, DH))
        msg_ref[slot, group * DH :, :] = pack_logs(wide)


def lin_pair_kernel(heads, backward, place, own_ref, rec_ref, out_ref):
    y = place[0]
    own_logs, rec_logs = read_logs(own_ref, heads), read_logs(rec_ref, heads)
    out_ref[heads * DH :, :] = pack_logs(own_logs + rec_logs)
    own_far = (y == 1) if backward else (y == 0)
    near_scale = jnp.exp(jnp.where(own_far, rec_logs, own_logs))
    own_scale = jnp.where(own_far, near_scale, 1.0)
    rec_scale = jnp.where(own_far, 1.0, near_scale)
    for i in range(heads):
        own, rec = own_ref[head_rows(i), :].astype(f32), rec_ref[head_rows(i), :].astype(f32)
        joint = own * own_scale[i : i + 1] + rec * rec_scale[i : i + 1]
        out_ref[head_rows(i), :] = joint.astype(bf16)


def lin_scan_kernel(heads, fold, count, backward, place, own_ref, rec_ref, *rest):
    far, outs = rest[:count], rest[count:]
    y = place[0]
    if fold > 1:
        own_logs, rec_logs = read_logs(own_ref, heads), read_logs(rec_ref, heads)
        own_near = (y == 1) if backward else (y == 0)
        near_scale = jnp.exp(jnp.where(own_near, own_logs, rec_logs))
    far_scales = []
    passed = jnp.zeros((heads, DH), f32)
    for s in range(count):
        far_scales.append(jnp.exp(passed))
        passed = passed + read_logs(far[s], heads)
    for i in range(heads):
        total = jnp.zeros((DH, DH), f32)
        for s in range(count):
            total = total + far_scales[s][i : i + 1] * far[s][head_rows(i), :].astype(f32)
        if fold == 1:
            outs[0][head_rows(i), :] = total.astype(bf16)
            continue
        own, rec = own_ref[head_rows(i), :].astype(f32), rec_ref[head_rows(i), :].astype(f32)
        beyond = jnp.where(own_near, own, rec) + near_scale[i : i + 1] * total
        outs[0][head_rows(i), :] = jnp.where(own_near, total, beyond).astype(bf16)
        outs[1][head_rows(i), :] = jnp.where(own_near, beyond, total).astype(bf16)


def pick_state(refs, h, group, y):
    i = h % group
    if len(refs) == 1:
        return refs[0][head_rows(i), :]
    own, rec = refs[0][head_rows(i), :].astype(f32), refs[1][head_rows(i), :].astype(f32)
    return jnp.where(y == h // group, own, rec).astype(bf16)


def lin_attend_kernel(
    heads, fold, place, row_ref, col_ref, query_ref, key_ref, value_ref, gate_ref, grad_ref, gain_ref, *rest
):
    states, (att_ref, stat_ref) = rest[:fold], rest[fold:]
    rows = query_ref.shape[0]
    y = place[0]
    causal = lax.broadcasted_iota(jnp.int32, (rows, rows), 0) >= lax.broadcasted_iota(
        jnp.int32, (rows, rows), 1
    )
    squares = jnp.zeros((rows, DH), f32)
    crosses = jnp.zeros((rows, DH), f32)
    for h in range(heads):
        query, key, value = (r[:, head_rows(h)] for r in (query_ref, key_ref, value_ref))
        col = col_ref[:, h : h + 1]
        decay = jnp.exp(jnp.where(causal, col - row_ref[h : h + 1, :], negative_fill))
        weights = (nt(query, key) * decay).astype(bf16)
        state = pick_state(states, h, heads // fold, y)
        att = nn(weights, value) + jnp.exp(col) * nn(query, state)
        att_ref[:, head_rows(h)] = att
        sig = jax.nn.sigmoid(gate_ref[:, head_rows(h)].astype(f32))
        scaled = grad_ref[:, head_rows(h)].astype(f32) * gain_ref[:, head_rows(h)] * sig
        squares = squares + att * att
        crosses = crosses + scaled * att
    stat_ref[...] = jnp.concatenate(
        (
            jnp.sum(squares.T, axis=0, keepdims=True),
            jnp.sum(crosses.T, axis=0, keepdims=True),
            jnp.zeros((6, rows), f32),
        ),
        axis=0,
    )


def lin_norm_kernel(
    heads, fold, width, place, row_ref, stat_ref, att_ref, gate_ref, grad_ref, gain_ref, query_ref, own_ref, oth_ref,
    out_ref, gate_grad_ref, att_grad_ref, msg_ref,
):
    y = place[0]
    rows = query_ref.shape[0]
    stats = jnp.concatenate((stat_ref[...], jnp.zeros((DH - 8, rows), f32)), axis=0).T
    scaling = lax.rsqrt(stats[:, 0:1] / width + 1e-05)
    cross = scaling * stats[:, 1:2] / width
    group = heads // fold
    lead = jnp.exp(row_ref[...])
    for g in range(fold):
        slot = lax.rem(g + y, fold) if fold > 1 else 0
        for i in range(group):
            h = g * group + i
            gain = gain_ref[:, head_rows(h)]
            sig = jax.nn.sigmoid(gate_ref[:, head_rows(h)].astype(f32))
            normed = att_ref[:, head_rows(h)] * scaling
            scaled = grad_ref[:, head_rows(h)].astype(f32) * gain * sig
            out_ref[:, head_rows(h)] = (normed * gain * sig).astype(bf16)
            gate_grad_ref[:, head_rows(h)] = (scaled * normed * (1.0 - sig)).astype(bf16)
            att_grad = (scaling * (scaled - normed * cross)).astype(bf16)
            att_grad_ref[:, head_rows(h)] = att_grad
            query_t = query_ref[:, head_rows(h)].astype(f32).T * lead[h : h + 1, :]
            msg_ref[slot, head_rows(i), :] = nn(query_t.astype(bf16), att_grad).astype(bf16)
    msg_ref[0, group * DH :, :] = own_ref[group * DH :, :]
    if fold > 1:
        msg_ref[1, group * DH :, :] = oth_ref[group * DH :, :]


def lin_grad_kernel(heads, fold, place, row_ref, col_ref, query_ref, key_ref, value_ref, att_grad_ref, *rest):
    states, back_states = rest[:fold], rest[fold : 2 * fold]
    query_grad_ref, key_grad_ref, value_grad_ref = rest[2 * fold :]
    y = place[0]
    rows = query_ref.shape[0]
    first = lax.broadcasted_iota(jnp.int32, (rows, rows), 0)
    second = lax.broadcasted_iota(jnp.int32, (rows, rows), 1)
    causal, causal_t = first >= second, first <= second
    for h in range(heads):
        query, key, value, grad = (
            r[:, head_rows(h)] for r in (query_ref, key_ref, value_ref, att_grad_ref)
        )
        col, row = col_ref[:, h : h + 1], row_ref[h : h + 1, :]
        decay = jnp.exp(jnp.where(causal, col - row, negative_fill))
        decay_t = jnp.exp(jnp.where(causal_t, row - col, negative_fill))
        lead, tail = jnp.exp(col), jnp.exp(row[:, rows - 1 : rows] - col)
        state = pick_state(states, h, heads // fold, y)
        back = pick_state(back_states, h, heads // fold, y)
        grad_weights = (nt(grad, value) * decay).astype(bf16)
        grad_weights_t = (nt(value, grad) * decay_t).astype(bf16)
        weights_t = (nt(key, query) * decay_t).astype(bf16)
        query_grad = nn(grad_weights, key) + lead * nt(grad, state)
        key_grad = nn(grad_weights_t, query) + tail * nt(value, back)
        value_grad = nn(weights_t, grad) + tail * nn(key, back)
        query_grad_ref[:, head_rows(h)] = query_grad.astype(bf16)
        key_grad_ref[:, head_rows(h)] = key_grad.astype(bf16)
        value_grad_ref[:, head_rows(h)] = value_grad.astype(bf16)


def diagonal_mask(y, keys, first, count, tokens, rows):
    key_at = lax.rem(lax.broadcasted_iota(jnp.int32, (keys, count), 0) + y * tokens, rows)
    query_at = lax.rem(lax.broadcasted_iota(jnp.int32, (keys, count), 1) + first + y * tokens, rows)
    return key_at <= query_at


def stack_rows(refs):
    parts = [r[...] for r in refs]
    return parts[0] if len(parts) == 1 else jnp.concatenate(parts, axis=0)


def soft_forward_kernel(fold, tokens, shift, first, last, place, *refs):
    refs = list(refs)
    take = lambda count: [refs.pop(0) for _ in range(count)]
    query_refs = take(fold)
    grad_refs = take(fold) if last else []
    (kv_ref,) = take(1)
    carry = take(0 if first else 3)
    outs = take(fold + 2 if last else 3)
    peak, total, acc = refs
    b = pl.program_id(1)
    rows = tokens * fold

    @pl.when(b == 0)
    def _():
        if first:
            peak[...] = jnp.full((1, rows), negative_fill, f32)
            total[...] = jnp.zeros((1, rows), f32)
            acc[...] = jnp.zeros((DH, rows), f32)
        else:
            peak[...], total[...], acc[...] = (r[0] for r in carry)

    @pl.when(place[1] >= shift + b)
    def _():
        key, value = kv_ref[0, :, :DH], kv_ref[0, :, DH:]
        query = stack_rows(query_refs)
        step = min(CHUNK, rows)
        for at in range(0, rows, step):
            span = slice(at, at + step)
            scores = nt(key, query[span]) * (LOG2E * DH**-0.5)
            if shift == 0:
                mask = diagonal_mask(place[0], rows, at, step, tokens, rows)
                scores = jnp.where(mask, scores, negative_fill)
            old = peak[:, span]
            fresh = jnp.maximum(old, jnp.max(scores, axis=0, keepdims=True))
            probs = jnp.exp2(scores - fresh)
            fade = jnp.exp2(old - fresh)
            peak[:, span] = fresh
            total[:, span] = total[:, span] * fade + jnp.sum(probs, axis=0, keepdims=True)
            acc[:, span] = acc[:, span] * fade + tn(value, probs.astype(bf16))

    @pl.when(b == pl.num_programs(1) - 1)
    def _():
        if not last:
            for out, value in zip(outs, (peak, total, acc)):
                out[0] = value[...]
            return
        out_t = (acc[...] / total[...]).astype(bf16).astype(f32)
        out = out_t.T.astype(bf16)
        for i in range(fold):
            outs[i][...] = out[i * tokens : (i + 1) * tokens]
        grad_t = stack_rows(grad_refs).astype(f32).T
        outs[fold][0] = peak[...] + jnp.log(total[...]) * LOG2E
        outs[fold + 1][0] = jnp.sum(grad_t * out_t, axis=0, keepdims=True)


def soft_specs(fold, tokens, group, head_of):
    own = pl.BlockSpec((tokens, DH), lambda *a: (0, a[-1][0] * group + head_of(*a)))
    rec = pl.BlockSpec((tokens, DH), lambda *a: (0, head_of(*a)))
    return [own, rec][:fold]


def soft_call(kernel, place, grid, in_specs, arrays, out_specs, outs, scratch, flops):
    moved = sum(a.size * a.dtype.itemsize for a in arrays)
    return pl.pallas_call(
        kernel,
        out_shape=outs,
        grid_spec=pltpu.PrefetchScalarGridSpec(
            num_scalar_prefetch=1,
            grid=grid,
            in_specs=in_specs,
            out_specs=out_specs,
            scratch_shapes=scratch,
        ),
        compiler_params=pltpu.CompilerParams(
            dimension_semantics=("arbitrary", "arbitrary"), vmem_limit_bytes=VMEM_BYTES
        ),
        cost_estimate=pl.CostEstimate(flops=flops, bytes_accessed=moved, transcendentals=0),
    )(place, *arrays)


def soft_forward(place, queries, grads, kv, shift, carry, last):
    fold, tokens = len(queries), queries[0].shape[0]
    group = queries[0].shape[1] // DH // fold
    blocks, rows = kv.shape[0], kv.shape[1]
    first = carry is None
    row_specs = soft_specs(fold, tokens, group, lambda h, b, p: h)
    line = pl.BlockSpec((1, 1, rows), lambda h, b, p: (h, 0, 0))
    tall = pl.BlockSpec((1, DH, rows), lambda h, b, p: (h, 0, 0))
    kv_spec = pl.BlockSpec((1, rows, 2 * DH), lambda h, b, p: (b, 0, 0))
    lines = jax.ShapeDtypeStruct((group, 1, rows), f32)
    talls = jax.ShapeDtypeStruct((group, DH, rows), f32)
    arrays, specs = list(queries), list(row_specs)
    if last:
        arrays, specs = arrays + list(grads), specs + row_specs
    arrays, specs = arrays + [kv], specs + [kv_spec]
    if not first:
        arrays, specs = arrays + list(carry), specs + [line, line, tall]
    if last:
        half = pl.BlockSpec((tokens, DH), lambda h, b, p: (0, h))
        out_specs = [half] * fold + [line, line]
        outs = [jax.ShapeDtypeStruct((tokens, group * DH), bf16)] * fold + [lines, lines]
    else:
        out_specs, outs = [line, line, tall], [lines, lines, talls]
    scratch = [pltpu.VMEM((1, rows), f32), pltpu.VMEM((1, rows), f32), pltpu.VMEM((DH, rows), f32)]
    kernel = functools.partial(soft_forward_kernel, fold, tokens, shift, first, last)
    flops = 4 * group * blocks * rows * rows * DH
    return soft_call(kernel, place, (group, blocks), specs, arrays, out_specs, outs, scratch, flops)


def soft_backward_kernel(fold, tokens, shift, first, last, place, *refs):
    refs = list(refs)
    take = lambda count: [refs.pop(0) for _ in range(count)]
    query_refs, grad_refs = take(fold), take(fold)
    log_ref, delta_ref, kv_ref = take(3)
    carry = take(0 if first else 1)
    (kv_grad_ref,) = take(1)
    outs = take(fold if last else 1)
    key_acc, value_acc, query_acc = refs
    b, h = pl.program_id(0), pl.program_id(1)
    rows = tokens * fold

    @pl.when(h == 0)
    def _():
        key_acc[...] = jnp.zeros((rows, DH), f32)
        value_acc[...] = jnp.zeros((rows, DH), f32)

    @pl.when(b == 0)
    def _():
        query_acc[h] = jnp.zeros((DH, rows), f32) if first else carry[0][0]

    @pl.when(place[1] >= shift + b)
    def _():
        key, value = kv_ref[0, :, :DH], kv_ref[0, :, DH:]
        query, grad = stack_rows(query_refs), stack_rows(grad_refs)
        step = min(CHUNK, rows)
        for at in range(0, rows, step):
            span = slice(at, at + step)
            scores = nt(key, query[span]) * (LOG2E * DH**-0.5) - log_ref[0, :, span]
            if shift == 0:
                mask = diagonal_mask(place[0], rows, at, step, tokens, rows)
                scores = jnp.where(mask, scores, negative_fill)
            probs = jnp.exp2(scores)
            score_grad = (probs * (nt(value, grad[span]) - delta_ref[0, :, span])).astype(bf16)
            value_acc[...] += nn(probs.astype(bf16), grad[span])
            key_acc[...] += nn(score_grad, query[span])
            query_acc[h, :, span] += tn(key, score_grad)

    @pl.when(h == pl.num_programs(1) - 1)
    def _():
        kv_grad_ref[0, :, :DH] = (key_acc[...] * DH**-0.5).astype(kv_grad_ref.dtype)
        kv_grad_ref[0, :, DH:] = value_acc[...].astype(kv_grad_ref.dtype)

    @pl.when(b == pl.num_programs(0) - 1)
    def _():
        if not last:
            outs[0][0] = query_acc[h]
            return
        query_grad = (query_acc[h] * DH**-0.5).T.astype(bf16)
        for i in range(fold):
            outs[i][...] = query_grad[i * tokens : (i + 1) * tokens]


def soft_backward(place, queries, grads, logs, deltas, kv, shift, carry, last):
    fold, tokens = len(queries), queries[0].shape[0]
    group = queries[0].shape[1] // DH // fold
    blocks, rows = kv.shape[0], kv.shape[1]
    first = carry is None
    row_specs = soft_specs(fold, tokens, group, lambda b, h, p: h)
    line = pl.BlockSpec((1, 1, rows), lambda b, h, p: (h, 0, 0))
    tall = pl.BlockSpec((1, DH, rows), lambda b, h, p: (h, 0, 0))
    kv_spec = pl.BlockSpec((1, rows, 2 * DH), lambda b, h, p: (b, 0, 0))
    arrays = list(queries) + list(grads) + [logs, deltas, kv]
    specs = row_specs + row_specs + [line, line, kv_spec]
    if not first:
        arrays, specs = arrays + [carry], specs + [tall]
    outs = [jax.ShapeDtypeStruct((blocks, rows, 2 * DH), f32 if last else bf16)]
    out_specs = [kv_spec]
    if last:
        half = pl.BlockSpec((tokens, DH), lambda b, h, p: (0, h))
        out_specs += [half] * fold
        outs += [jax.ShapeDtypeStruct((tokens, group * DH), bf16)] * fold
    else:
        out_specs += [tall]
        outs += [jax.ShapeDtypeStruct((group, DH, rows), f32)]
    scratch = [
        pltpu.VMEM((rows, DH), f32),
        pltpu.VMEM((rows, DH), f32),
        pltpu.VMEM((group, DH, rows), f32),
    ]
    kernel = functools.partial(soft_backward_kernel, fold, tokens, shift, first, last)
    flops = 10 * group * blocks * rows * rows * DH
    return soft_call(kernel, place, (blocks, group), specs, arrays, out_specs, outs, scratch, flops)


def body(
    lin_query,
    lin_key,
    lin_value,
    log_decay,
    norm_gain,
    lin_gate,
    lin_grad,
    soft_query,
    soft_key,
    soft_value,
    soft_grad,
):
    count = lax.axis_size("ctx")
    kv_heads = soft_key.shape[1] // DH
    fold = 2 if kv_heads == 2 and count % 2 == 0 else 1
    laps = count // fold
    index = lax.axis_index("ctx")
    y, z = lax.rem(index, fold), lax.div(index, fold)
    place = jnp.stack((y, z)).astype(jnp.int32)
    tokens = soft_query.shape[0]
    rows = tokens * fold
    heads = lin_query.shape[1] // DH
    group = heads // fold
    width = lin_query.shape[1] * lax.axis_size("tp")
    gain = norm_gain[None, :]

    def swap(a):
        return lax.ppermute(a, "ctx", [(i, i ^ 1) for i in range(count)])

    def up(a, s):
        return lax.ppermute(a, "ctx", [(i, i + fold * s) for i in range(count - fold * s)])

    def down(a, s):
        return lax.ppermute(a, "ctx", [(i + fold * s, i) for i in range(count - fold * s)])

    def columns(a, part):
        size = a.shape[1] // fold
        return lax.dynamic_slice_in_dim(a, part * size, size, 1) if fold > 1 else a

    def joined(own, rec):
        if fold == 1:
            return own
        low, high = jnp.where(y == 0, own, rec), jnp.where(y == 0, rec, own)
        return jnp.concatenate((low, high), axis=1)

    kv = jnp.concatenate((columns(soft_key, y), columns(soft_value, y)), axis=1)
    queries, grads = [soft_query], [soft_grad]
    if fold > 1:
        kv_sent = jnp.concatenate((columns(soft_key, 1 - y), columns(soft_value, 1 - y)), axis=1)
        kv = jnp.concatenate((kv, swap(kv_sent)), axis=0)
        queries.append(swap(columns(soft_query, 1 - y)))
        grads.append(swap(columns(soft_grad, 1 - y)))
    stack = laps > 8
    kv_far = [up(kv, s) for s in range(1, laps)]

    msg_rows = group * DH + extra_rows(group)
    msg = jax.ShapeDtypeStruct((msg_rows, DH), bf16)
    msgs = jax.ShapeDtypeStruct((fold, msg_rows, DH), bf16)
    state = jax.ShapeDtypeStruct((group * DH, DH), bf16)
    flat = jax.ShapeDtypeStruct((tokens, heads * DH), bf16)
    state_msgs, log_rows, log_cols = whole_call(
        functools.partial(lin_state_kernel, heads, fold),
        place,
        (log_decay, lin_key, lin_value),
        [
            msgs,
            jax.ShapeDtypeStruct((heads, tokens), f32),
            jax.ShapeDtypeStruct((tokens, heads), f32),
        ],
        2 * heads * tokens * DH * DH,
    )

    def carry_over(own, other, backward):
        rec = swap(other) if fold > 1 else own
        joint = own
        if fold > 1:
            (joint,) = whole_call(
                functools.partial(lin_pair_kernel, group, backward), place, (own, rec), [msg]
            )
        far = [(down if backward else up)(joint, s) for s in range(1, laps)]
        got = whole_call(
            functools.partial(lin_scan_kernel, group, fold, laps - 1, backward),
            place,
            (own, rec, *far),
            [state] * fold,
        )
        return (got[0], swap(got[1])) if fold > 1 else tuple(got)

    own_msg, oth_msg = state_msgs[0], state_msgs[fold - 1]
    carried = carry_over(own_msg, oth_msg, False)
    square = 2 * heads * tokens * tokens * DH
    attended, stats = whole_call(
        functools.partial(lin_attend_kernel, heads, fold),
        place,
        (log_rows, log_cols, lin_query, lin_key, lin_value, lin_gate, lin_grad, gain, *carried),
        [
            jax.ShapeDtypeStruct((tokens, heads * DH), f32),
            jax.ShapeDtypeStruct((8, tokens), f32),
        ],
        3 * square,
    )
    stats = lax.psum(stats, "tp")
    lin_out, lin_gate_grad, att_grad, back_msgs = whole_call(
        functools.partial(lin_norm_kernel, heads, fold, width),
        place,
        (log_rows, stats, attended, lin_gate, lin_grad, gain, lin_query, own_msg, oth_msg),
        [flat, flat, flat, msgs],
        square,
    )
    returned = carry_over(back_msgs[0], back_msgs[fold - 1], True)
    lin_query_grad, lin_key_grad, lin_value_grad = whole_call(
        functools.partial(lin_grad_kernel, heads, fold),
        place,
        (log_rows, log_cols, lin_query, lin_key, lin_value, att_grad, *carried, *returned),
        [flat, flat, flat],
        8 * square,
    )

    if stack:
        steps = [(0, kv[None]), (1, jnp.stack(kv_far))]
    else:
        steps = [(s, a[None]) for s, a in enumerate([kv] + kv_far)]
    carry = None
    for s, blocks in steps:
        carry = soft_forward(place, queries, grads, blocks, s, carry, s == steps[-1][0])
    outs, (logs, deltas) = carry[:fold], carry[fold:]
    carry = None
    terms = []
    for s, blocks in steps[::-1]:
        kv_grad, *carry = soft_backward(
            place, queries, grads, logs, deltas, blocks, s, carry[0] if carry else None, s == 0
        )
        if s > 0:
            terms += [down(kv_grad[i], s + i) for i in range(blocks.shape[0])]
    total = kv_grad[0]
    for term in terms:
        total = total + term.astype(f32)
    total = total.astype(bf16)
    kv_own = total[:tokens]
    kv_rec = swap(total[tokens:]) if fold > 1 else None
    if fold > 1:
        soft_out = joined(outs[0], swap(outs[1]))
        soft_query_grad = joined(carry[0], swap(carry[1]))
        soft_key_grad = joined(kv_own[:, :DH], kv_rec[:, :DH])
        soft_value_grad = joined(kv_own[:, DH:], kv_rec[:, DH:])
    else:
        soft_out, soft_query_grad = outs[0], carry[0]
        soft_key_grad, soft_value_grad = kv_own[:, :DH], kv_own[:, DH:]
    return (
        lin_out,
        lin_query_grad,
        lin_key_grad,
        lin_value_grad,
        lin_gate_grad,
        soft_out,
        soft_query_grad,
        soft_key_grad,
        soft_value_grad,
    )


def solution(mesh):
    spread = P("ctx", "tp")
    return jax.shard_map(
        body,
        mesh=mesh,
        in_specs=(spread, spread, spread, P("tp", "ctx"), P("tp")) + (spread,) * 6,
        out_specs=(spread,) * 9,
        check_vma=False,
    )
```

```python
import functools

import jax
import jax.numpy as jnp
from jax import lax
from jax.experimental import pallas as pl
from jax.experimental.pallas import tpu as pltpu
from jax.sharding import PartitionSpec as P

DH = 128
LOG2E = 1.4426950408889634
LN2 = 0.6931471805599453
negative_fill = -1e30
f32 = jnp.float32
bf16 = jnp.bfloat16
VMEM_BYTES = 24 * 1024 * 1024
FORWARD_CHUNK = 128
FLOPS_PER_MICRO = 1150 * 10**6
BACKWARD_CHUNK = 256

SMEM_SPEC = pl.BlockSpec(memory_space=pltpu.SMEM)
VMEM_SPEC = pl.BlockSpec(memory_space=pltpu.VMEM)
ANY_SPEC = pl.BlockSpec(memory_space=pl.ANY)


def nn(a, b):
    return jnp.dot(a, b, preferred_element_type=f32)


def nt(a, b):
    return lax.dot_general(a, b, (((1,), (1,)), ((), ())), preferred_element_type=f32)


def tn(a, b):
    return lax.dot_general(a, b, (((0,), (0,)), ((), ())), preferred_element_type=f32)


def whole_call(kernel, place, arrays, outs, micros, after=(), aliases={}, scratch=()):
    def ordered(place, *refs):
        kernel(place, *refs[: len(arrays)], *refs[len(arrays) + len(after) :])

    return pl.pallas_call(
        ordered,
        out_shape=outs,
        in_specs=[SMEM_SPEC] + [VMEM_SPEC] * len(arrays) + [ANY_SPEC] * len(after),
        out_specs=[VMEM_SPEC] * len(outs),
        scratch_shapes=list(scratch),
        input_output_aliases={i + 1: o for i, o in aliases.items()},
        compiler_params=pltpu.CompilerParams(vmem_limit_bytes=VMEM_BYTES),
        cost_estimate=pl.CostEstimate(
            flops=int(micros * FLOPS_PER_MICRO), bytes_accessed=1, transcendentals=0
        ),
    )(place, *arrays, *after)


def split3(x):
    hi = x.astype(bf16)
    rest = x - hi.astype(f32)
    lo = rest.astype(bf16)
    return hi, lo, (rest - lo.astype(f32)).astype(bf16)


def extra_rows(heads):
    return 16 * pl.cdiv(3 * heads, 16)


def pack_logs(rows):
    heads = rows.shape[0]
    pad = extra_rows(heads) - 3 * heads
    parts = [p.astype(f32) for p in split3(rows)]
    if pad:
        parts.append(jnp.zeros((pad, DH), f32))
    return jnp.concatenate(parts, axis=0).astype(bf16)


def read_logs(ref, heads):
    part = ref[heads * DH :, :].astype(f32)
    return part[:heads] + part[heads : 2 * heads] + part[2 * heads : 3 * heads]


def head_rows(h):
    return slice(h * DH, (h + 1) * DH)


def lin_state_kernel(heads, fold, place, log_ref, key_ref, value_ref, msg_ref, row_ref, col_ref):
    rows = key_ref.shape[0]
    y = place[0]
    later = lax.broadcasted_iota(jnp.int32, (rows, rows), 0)
    earlier = lax.broadcasted_iota(jnp.int32, (rows, rows), 1)
    tri = (earlier <= later).astype(f32)
    logs = log_ref[...]
    exact = lax.Precision.HIGHEST
    dims = (((1,), (1,)), ((), ()))
    by_row = lax.dot_general(logs, tri, dims, precision=exact, preferred_element_type=f32)
    by_col = lax.dot_general(tri, logs, dims, precision=exact, preferred_element_type=f32)
    row_ref[...] = by_row
    col_ref[...] = by_col
    totals = by_row[:, rows - 1 : rows]
    tail = jnp.exp(totals - by_row)
    group = heads // fold
    for g in range(fold):
        slot = lax.rem(g + y, fold) if fold > 1 else 0
        for i in range(group):
            h = g * group + i
            key_t = key_ref[:, head_rows(h)].astype(f32).T * tail[h : h + 1, :]
            state = nn(key_t.astype(bf16), value_ref[:, head_rows(h)])
            msg_ref[slot, head_rows(i), :] = state.astype(bf16)
        wide = jnp.broadcast_to(totals[g * group : (g + 1) * group], (group, DH))
        msg_ref[slot, group * DH :, :] = pack_logs(wide)


def lin_pair_kernel(heads, backward, place, own_ref, rec_ref, out_ref):
    y = place[0]
    own_logs, rec_logs = read_logs(own_ref, heads), read_logs(rec_ref, heads)
    out_ref[heads * DH :, :] = pack_logs(own_logs + rec_logs)
    own_far = (y == 1) if backward else (y == 0)
    near_scale = jnp.exp(jnp.where(own_far, rec_logs, own_logs))
    own_scale = jnp.where(own_far, near_scale, 1.0)
    rec_scale = jnp.where(own_far, 1.0, near_scale)
    for i in range(heads):
        own, rec = own_ref[head_rows(i), :].astype(f32), rec_ref[head_rows(i), :].astype(f32)
        joint = own * own_scale[i : i + 1] + rec * rec_scale[i : i + 1]
        out_ref[head_rows(i), :] = joint.astype(bf16)


def lin_combine_kernel(heads, place, own_ref, rec_ref, out_ref):
    own_logs = read_logs(own_ref, heads)
    out_ref[heads * DH :, :] = pack_logs(own_logs + read_logs(rec_ref, heads))
    scale = jnp.exp(own_logs)
    for i in range(heads):
        own, rec = own_ref[head_rows(i), :].astype(f32), rec_ref[head_rows(i), :].astype(f32)
        out_ref[head_rows(i), :] = (own + rec * scale[i : i + 1]).astype(bf16)


def lin_scan_kernel(heads, fold, count, backward, place, own_ref, rec_ref, *rest):
    far, outs = rest[:count], rest[count:]
    y = place[0]
    if fold > 1:
        own_logs, rec_logs = read_logs(own_ref, heads), read_logs(rec_ref, heads)
        own_near = (y == 1) if backward else (y == 0)
        near_scale = jnp.exp(jnp.where(own_near, own_logs, rec_logs))
    far_scales = []
    passed = jnp.zeros((heads, DH), f32)
    for s in range(count):
        far_scales.append(jnp.exp(passed))
        passed = passed + read_logs(far[s], heads)
    for i in range(heads):
        total = jnp.zeros((DH, DH), f32)
        for s in range(count):
            total = total + far_scales[s][i : i + 1] * far[s][head_rows(i), :].astype(f32)
        if fold == 1:
            outs[0][head_rows(i), :] = total.astype(bf16)
            continue
        own, rec = own_ref[head_rows(i), :].astype(f32), rec_ref[head_rows(i), :].astype(f32)
        beyond = jnp.where(own_near, own, rec) + near_scale[i : i + 1] * total
        outs[0][head_rows(i), :] = jnp.where(own_near, total, beyond).astype(bf16)
        outs[1][head_rows(i), :] = jnp.where(own_near, beyond, total).astype(bf16)


def pick_state(refs, h, group, y):
    i = h % group
    if len(refs) == 1:
        return refs[0][head_rows(i), :]
    own, rec = refs[0][head_rows(i), :].astype(f32), refs[1][head_rows(i), :].astype(f32)
    return jnp.where(y == h // group, own, rec).astype(bf16)


def lin_attend_kernel(
    heads, fold, place, row_ref, col_ref, query_ref, key_ref, value_ref, gate_ref, grad_ref, gain_ref, *rest
):
    states, (att_ref, stat_ref) = rest[:fold], rest[fold:]
    rows = query_ref.shape[0]
    y = place[0]
    causal = lax.broadcasted_iota(jnp.int32, (rows, rows), 0) >= lax.broadcasted_iota(
        jnp.int32, (rows, rows), 1
    )
    squares = jnp.zeros((rows, DH), f32)
    crosses = jnp.zeros((rows, DH), f32)
    for h in range(heads):
        query, key, value = (r[:, head_rows(h)] for r in (query_ref, key_ref, value_ref))
        col = col_ref[:, h : h + 1]
        decay = jnp.exp(jnp.where(causal, col - row_ref[h : h + 1, :], negative_fill))
        weights = (nt(query, key) * decay).astype(bf16)
        state = pick_state(states, h, heads // fold, y)
        att = nn(weights, value) + jnp.exp(col) * nn(query, state)
        att_ref[:, head_rows(h)] = att
        sig = jax.nn.sigmoid(gate_ref[:, head_rows(h)].astype(f32))
        scaled = grad_ref[:, head_rows(h)].astype(f32) * gain_ref[:, head_rows(h)] * sig
        squares = squares + att * att
        crosses = crosses + scaled * att
    stat_ref[...] = jnp.concatenate(
        (
            jnp.sum(squares.T, axis=0, keepdims=True),
            jnp.sum(crosses.T, axis=0, keepdims=True),
            jnp.zeros((6, rows), f32),
        ),
        axis=0,
    )


def lin_norm_kernel(
    heads, fold, width, place, row_ref, att_ref, gate_ref, grad_ref, gain_ref, query_ref, own_ref, oth_ref, *rest
):
    *stat_refs, out_ref, gate_grad_ref, att_grad_ref, msg_ref = rest
    y = place[0]
    rows = query_ref.shape[0]
    stats = sum((r[...] for r in stat_refs[1:]), stat_refs[0][...])
    stats = jnp.concatenate((stats, jnp.zeros((DH - 8, rows), f32)), axis=0).T
    scaling = lax.rsqrt(stats[:, 0:1] / width + 1e-05)
    cross = scaling * stats[:, 1:2] / width
    group = heads // fold
    lead = jnp.exp(row_ref[...])
    for g in range(fold):
        slot = lax.rem(g + y, fold) if fold > 1 else 0
        for i in range(group):
            h = g * group + i
            gain = gain_ref[:, head_rows(h)]
            sig = jax.nn.sigmoid(gate_ref[:, head_rows(h)].astype(f32))
            normed = att_ref[:, head_rows(h)] * scaling
            scaled = grad_ref[:, head_rows(h)].astype(f32) * gain * sig
            out_ref[:, head_rows(h)] = (normed * gain * sig).astype(bf16)
            gate_grad_ref[:, head_rows(h)] = (scaled * normed * (1.0 - sig)).astype(bf16)
            att_grad = (scaling * (scaled - normed * cross)).astype(bf16)
            att_grad_ref[:, head_rows(h)] = att_grad
            query_t = query_ref[:, head_rows(h)].astype(f32).T * lead[h : h + 1, :]
            msg_ref[slot, head_rows(i), :] = nn(query_t.astype(bf16), att_grad).astype(bf16)
    msg_ref[0, group * DH :, :] = own_ref[group * DH :, :]
    if fold > 1:
        msg_ref[1, group * DH :, :] = oth_ref[group * DH :, :]


def lin_local_kernel(heads, fold, place, row_ref, col_ref, query_ref, key_ref, value_ref, att_grad_ref, *rest):
    states, (query_grad_ref, key_part_ref, value_part_ref) = rest[:fold], rest[fold:]
    y = place[0]
    rows = query_ref.shape[0]
    first = lax.broadcasted_iota(jnp.int32, (rows, rows), 0)
    second = lax.broadcasted_iota(jnp.int32, (rows, rows), 1)
    causal, causal_t = first >= second, first <= second
    for h in range(heads):
        query, key, value, grad = (
            r[:, head_rows(h)] for r in (query_ref, key_ref, value_ref, att_grad_ref)
        )
        col, row = col_ref[:, h : h + 1], row_ref[h : h + 1, :]
        decay = jnp.exp(jnp.where(causal, col - row, negative_fill))
        decay_t = jnp.exp(jnp.where(causal_t, row - col, negative_fill))
        state = pick_state(states, h, heads // fold, y)
        grad_weights = (nt(grad, value) * decay).astype(bf16)
        grad_weights_t = (nt(value, grad) * decay_t).astype(bf16)
        weights_t = (nt(key, query) * decay_t).astype(bf16)
        query_grad = nn(grad_weights, key) + jnp.exp(col) * nt(grad, state)
        query_grad_ref[:, head_rows(h)] = query_grad.astype(bf16)
        key_part_ref[:, head_rows(h)] = nn(grad_weights_t, query)
        value_part_ref[:, head_rows(h)] = nn(weights_t, grad)


def final_kernel(heads, fold, place, row_ref, col_ref, key_ref, value_ref, key_part_ref, value_part_ref, *rest):
    states, rest = rest[:fold], rest[fold:]
    halves, outs = rest[:-6], rest[-6:]
    y = place[0]
    rows = key_ref.shape[0]
    for h in range(heads):
        key, value = key_ref[:, head_rows(h)], value_ref[:, head_rows(h)]
        tail = jnp.exp(row_ref[h : h + 1, rows - 1 : rows] - col_ref[:, h : h + 1])
        state = pick_state(states, h, heads // fold, y)
        key_grad = key_part_ref[:, head_rows(h)] + tail * nt(value, state)
        value_grad = value_part_ref[:, head_rows(h)] + tail * nn(key, state)
        outs[0][:, head_rows(h)] = key_grad.astype(bf16)
        outs[1][:, head_rows(h)] = value_grad.astype(bf16)
    count = len(halves) // 3
    for i in range(fold):
        at = (y + i) % fold
        for out, part in ((outs[2], halves[i]), (outs[3], halves[count + i])):
            size = part.shape[1]
            out[:, pl.ds(pl.multiple_of(at * size, DH), size)] = part[...]
        part = halves[2 * count + i]
        for j in range(2):
            there = pl.ds(pl.multiple_of(at * DH, DH), DH)
            outs[4 + j][:, there] = part[:rows, j * DH : (j + 1) * DH]


def diagonal_mask(y, keys, first, count, tokens, rows):
    key_at = lax.rem(lax.broadcasted_iota(jnp.int32, (keys, count), 0) + y * tokens, rows)
    query_at = lax.rem(lax.broadcasted_iota(jnp.int32, (keys, count), 1) + first + y * tokens, rows)
    return key_at <= query_at


def soft_pack_kernel(place, rows_ref, out_ref):
    half = rows_ref.shape[1] // 2
    out_ref[...] = rows_ref[:, pl.ds(pl.multiple_of((1 - place[0]) * half, DH), half)]


def head_of_rows(y, group, h, own_ref, rec_ref):
    if rec_ref is None:
        return own_ref[:, head_rows(h)]
    own = own_ref[:, pl.ds(pl.multiple_of((y * group + h) * DH, DH), DH)]
    return jnp.concatenate((own, rec_ref[:, head_rows(h)]), axis=0)


def soft_forward_kernel(fold, tokens, group, diagonal, last, place, *refs):
    refs = list(refs)
    take = lambda count: [refs.pop(0) for _ in range(count)]
    query_ref = take(1)[0]
    kv_refs = take(fold)
    grad_ref = take(1)[0] if last else None
    query_rec = take(1)[0] if fold > 1 else None
    grad_rec = take(1)[0] if fold > 1 and last else None
    old_peak, old_total, old_acc = take(3) if not diagonal else (None,) * 3
    outs = take(fold + 2 if last else 3)
    peak, total, acc = refs if last else outs
    y = place[0]
    rows = tokens * fold

    def compute():
        kv = jnp.concatenate([r[...] for r in kv_refs], axis=0)
        key, value = kv[:, :DH], kv[:, DH:]
        step = min(FORWARD_CHUNK, rows)
        for h in range(group):
            query = head_of_rows(y, group, h, query_ref, query_rec)
            for at in range(0, rows, step):
                span = slice(at, at + step)
                scores = nt(key, query[span]) * (LOG2E * DH**-0.5)
                if diagonal:
                    mask = diagonal_mask(y, rows, at, step, tokens, rows)
                    scores = jnp.where(mask, scores, negative_fill)
                    fresh = jnp.max(scores, axis=0, keepdims=True)
                    probs = jnp.exp2(scores - fresh)
                    total[h, :, span] = jnp.sum(probs, axis=0, keepdims=True)
                    acc[h, :, span] = tn(value, probs.astype(bf16))
                else:
                    old = old_peak[h, :, span]
                    fresh = jnp.maximum(old, jnp.max(scores, axis=0, keepdims=True))
                    probs = jnp.exp2(scores - fresh)
                    fade = jnp.exp2(old - fresh)
                    total[h, :, span] = old_total[h, :, span] * fade + jnp.sum(
                        probs, axis=0, keepdims=True
                    )
                    acc[h, :, span] = old_acc[h, :, span] * fade + tn(value, probs.astype(bf16))
                peak[h, :, span] = fresh

    if diagonal:
        compute()
    else:
        reached = place[1] >= place[2]
        pl.when(reached)(compute)
        if last:

            @pl.when(jnp.logical_not(reached))
            def _():
                peak[...], total[...], acc[...] = old_peak[...], old_total[...], old_acc[...]

    if last:
        for h in range(group):
            out_t = (acc[h] / total[h]).astype(bf16).astype(f32)
            out = out_t.T.astype(bf16)
            for i in range(fold):
                outs[i][:, head_rows(h)] = out[i * tokens : (i + 1) * tokens]
            grad_t = head_of_rows(y, group, h, grad_ref, grad_rec).astype(f32).T
            outs[fold][h] = peak[h] + jnp.log(total[h]) * LOG2E
            outs[fold + 1][h] = jnp.sum(grad_t * out_t, axis=0, keepdims=True)


def soft_forward(place, query, grad, rec, kv, carry, last, after=()):
    tokens, fold = query.shape[0], len(kv)
    rows, group = tokens * fold, query.shape[1] // DH // fold
    diagonal = carry is None
    lines = jax.ShapeDtypeStruct((group, 1, rows), f32)
    talls = jax.ShapeDtypeStruct((group, DH, rows), f32)
    own = (query, *kv, grad) if last else (query, *kv)
    arrays = (*own, *(rec if last else rec[:1]), *(() if diagonal else carry))
    aliases, scratch = {}, ()
    if last:
        outs = [jax.ShapeDtypeStruct((tokens, group * DH), bf16)] * fold + [lines, lines]
        scratch = [pltpu.VMEM(a.shape, f32) for a in (lines, lines, talls)]
    else:
        outs = [lines, lines, talls]
        if not diagonal:
            aliases = {len(arrays) - 3 + i: i for i in range(3)}
    kernel = functools.partial(soft_forward_kernel, fold, tokens, group, diagonal, last)
    return whole_call(kernel, place, arrays, outs, 3.0 if last else 2.6, after, aliases, scratch)


def soft_backward_kernel(fold, tokens, group, diagonal, first, place, *refs):
    refs = list(refs)
    take = lambda count: [refs.pop(0) for _ in range(count)]
    query_ref, grad_ref, log_ref, delta_ref = take(4)
    kv_refs = take(fold)
    query_rec, grad_rec = take(2) if fold > 1 else (None, None)
    old_acc = take(1)[0] if not first else None
    kv_grad_ref, *outs = refs
    y = place[0]
    rows = tokens * fold

    def compute():
        kv = jnp.concatenate([r[...] for r in kv_refs], axis=0)
        key, value = kv[:, :DH], kv[:, DH:]
        step = min(BACKWARD_CHUNK, rows)
        key_acc, value_acc = jnp.zeros((rows, DH), f32), jnp.zeros((rows, DH), f32)
        for h in range(group):
            query = head_of_rows(y, group, h, query_ref, query_rec)
            grad = head_of_rows(y, group, h, grad_ref, grad_rec)
            for at in range(0, rows, step):
                span = slice(at, at + step)
                scores = nt(key, query[span]) * (LOG2E * DH**-0.5) - log_ref[h, :, span]
                if diagonal:
                    mask = diagonal_mask(y, rows, at, step, tokens, rows)
                    scores = jnp.where(mask, scores, negative_fill)
                probs = jnp.exp2(scores)
                score_grad = (probs * (nt(value, grad[span]) - delta_ref[h, :, span])).astype(bf16)
                value_acc += nn(probs.astype(bf16), grad[span])
                key_acc += nn(score_grad, query[span])
                query_grad = tn(key, score_grad)
                if not first:
                    query_grad += old_acc[h, :, span]
                if diagonal:
                    query_grad = (query_grad * DH**-0.5).T.astype(bf16)
                    i, begin = at // tokens, at % tokens
                    outs[i][begin : begin + step, head_rows(h)] = query_grad
                else:
                    outs[0][h, :, span] = query_grad
        kv_grad_ref[:, :DH] = key_acc * DH**-0.5
        kv_grad_ref[:, DH:] = value_acc

    if diagonal:
        compute()
        return
    reached = place[1] >= place[2]
    pl.when(reached)(compute)

    @pl.when(jnp.logical_not(reached))
    def _():
        kv_grad_ref[...] = jnp.zeros_like(kv_grad_ref)
        if first:
            outs[0][...] = jnp.zeros_like(outs[0])


def soft_backward(place, query, grad, rec, logs, deltas, kv, carry, diagonal, after=()):
    tokens, fold = query.shape[0], len(kv)
    rows, group = tokens * fold, query.shape[1] // DH // fold
    first = carry is None
    arrays = (query, grad, logs, deltas, *kv, *rec, *(() if first else (carry,)))
    outs = [jax.ShapeDtypeStruct((rows, 2 * DH), f32)]
    aliases = {}
    if diagonal:
        outs += [jax.ShapeDtypeStruct((tokens, group * DH), bf16)] * fold
    else:
        outs += [jax.ShapeDtypeStruct((group, DH, rows), f32)]
        if not first:
            aliases = {len(arrays) - 1: 1}
    kernel = functools.partial(soft_backward_kernel, fold, tokens, group, diagonal, first)
    return whole_call(kernel, place, arrays, outs, 3.4, after, aliases)


def body(
    lin_query,
    lin_key,
    lin_value,
    log_decay,
    norm_gain,
    lin_gate,
    lin_grad,
    soft_query,
    soft_key,
    soft_value,
    soft_grad,
):
    count = lax.axis_size("ctx")
    kv_heads = soft_key.shape[1] // DH
    fold = 2 if kv_heads == 2 and count % 2 == 0 else 1
    laps = count // fold
    index = lax.axis_index("ctx")
    y, z = lax.rem(index, fold), lax.div(index, fold)
    place = jnp.stack((y, z)).astype(jnp.int32)
    tokens = soft_query.shape[0]
    rows = tokens * fold
    heads = lin_query.shape[1] // DH
    group = heads // fold
    width = lin_query.shape[1] * lax.axis_size("tp")
    gain = norm_gain[None, :]

    def swap(a):
        return lax.ppermute(a, "ctx", [(i, i ^ 1) for i in range(count)])

    def up(a, s):
        return lax.ppermute(a, "ctx", [(i, i + fold * s) for i in range(count - fold * s)])

    def down(a, s):
        return lax.ppermute(a, "ctx", [(i + fold * s, i) for i in range(count - fold * s)])

    def own_columns(a):
        size = a.shape[1] // 2
        return a if fold == 1 else jnp.where(y == 0, a[:, :size], a[:, size:])

    def partner_columns(a):
        size = a.shape[1] // 2
        return jnp.where(y == 0, a[:, size:], a[:, :size])

    def each(move, parts, s):
        return [move(a, s) for a in parts]

    def at_lap(s):
        return jnp.concatenate((place, jnp.asarray(s, jnp.int32)[None]))

    early = ()
    kv = [jnp.concatenate((own_columns(soft_key), own_columns(soft_value)), axis=1)]
    if fold > 1:
        kv_sent = jnp.concatenate((partner_columns(soft_key), partner_columns(soft_value)), axis=1)
        kv.append(swap(kv_sent))
        early = (kv_sent, kv[0])

    msg_rows = group * DH + extra_rows(group)
    msg = jax.ShapeDtypeStruct((msg_rows, DH), bf16)
    msgs = jax.ShapeDtypeStruct((fold, msg_rows, DH), bf16)
    state = jax.ShapeDtypeStruct((group * DH, DH), bf16)
    flat = jax.ShapeDtypeStruct((tokens, heads * DH), bf16)
    state_msgs, log_rows, log_cols = whole_call(
        functools.partial(lin_state_kernel, heads, fold),
        place,
        (log_decay, lin_key, lin_value),
        [
            msgs,
            jax.ShapeDtypeStruct((heads, tokens), f32),
            jax.ShapeDtypeStruct((tokens, heads), f32),
        ],
        1.4,
        early,
    )
    own_msg, oth_msg = state_msgs[0], state_msgs[fold - 1]
    rec = ()
    if fold > 1:
        half = jax.ShapeDtypeStruct((tokens, group * DH), bf16)
        (sent,) = whole_call(soft_pack_kernel, place, (soft_query,), [half], 0.6, (state_msgs,))
        rec = (swap(sent),)
    unrolled = laps <= 8
    if unrolled:
        kvs = [kv]
        for s in range(1, laps):
            kvs.append(each(up, kvs[-1], 1))

    def pair_states(own, other, backward, after=()):
        if fold == 1:
            return own, (own, own)
        rec = swap(other)
        kernel = functools.partial(lin_pair_kernel, group, backward)
        return whole_call(kernel, place, (own, rec), [msg], 0.6, after)[0], (own, rec)

    def send_states(joint, backward, after=()):
        got, step, move = [], 1, down if backward else up
        while step < laps:
            got.append(move(joint, step))
            step *= 2
            if step < laps:
                kernel = functools.partial(lin_combine_kernel, group)
                (joint,) = whole_call(kernel, place, (joint, got[-1]), [msg], 0.6, after)
        return joint, got

    def take_states(sent, backward, after=()):
        got = whole_call(
            functools.partial(lin_scan_kernel, group, fold, len(sent) - 2, backward),
            place,
            sent,
            [state] * fold,
            0.7,
            after=after,
        )
        return got[0], ((got[0], swap(got[1])) if fold > 1 else tuple(got))

    def forward(kv, s, carry, last, after=()):
        return soft_forward(at_lap(s), soft_query, soft_grad, rec, kv, carry, last, after)

    def backward(kv, s, carry, after=()):
        whole = (soft_query, soft_grad, rec, logs, deltas, kv, carry)
        return soft_backward(at_lap(s), *whole, isinstance(s, int) and s == 0, after)

    joint, pair = pair_states(own_msg, oth_msg, False)
    soft = forward(kv, 0, None, False)
    if fold > 1:
        (grad_sent,) = whole_call(soft_pack_kernel, place, (soft_grad,), [half], 0.6, (joint,))
        rec += (swap(grad_sent),)
    joint, far = send_states(joint, False)
    if unrolled:
        for s in range(1, laps - 1):
            soft = forward(kvs[s], s, soft, False)
        last_kv = kvs[-1]
    else:

        def far_forward(state, s):
            kv, soft = state
            kv = each(up, kv, 1)
            return (kv, forward(kv, s, soft, False)), kv

        (last_kv, soft), far_kvs = lax.scan(far_forward, (kv, soft), jnp.arange(1, laps - 1))
        last_kv = each(up, last_kv, 1)
    soft = forward(last_kv, laps - 1, soft, True)
    outs, (logs, deltas) = soft[:fold], soft[fold:]
    kept, carried = take_states((*pair, *far), False, (logs,))

    def added(kv_grad, hop):
        return (kv_grad + hop.astype(f32)).astype(bf16)

    kv_grad, carry = backward(last_kv, laps - 1, None)
    hop = down(kv_grad.astype(bf16), 1)

    attended, stats = whole_call(
        functools.partial(lin_attend_kernel, heads, fold),
        place,
        (log_rows, log_cols, lin_query, lin_key, lin_value, lin_gate, lin_grad, gain, *carried),
        [
            jax.ShapeDtypeStruct((tokens, heads * DH), f32),
            jax.ShapeDtypeStruct((8, tokens), f32),
        ],
        2.0,
    )
    tp = lax.axis_size("tp")
    if tp <= 4 and tp & (tp - 1) == 0:
        all_stats = [stats] + [
            lax.ppermute(stats, "tp", [(i, i ^ k) for i in range(tp)]) for k in range(1, tp)
        ]
    else:
        all_stats = [lax.psum(stats, "tp")]

    def norm(after):
        return whole_call(
            functools.partial(lin_norm_kernel, heads, fold, width),
            place,
            (log_rows, attended, lin_gate, lin_grad, gain, lin_query, own_msg, oth_msg, *all_stats),
            [flat, flat, flat, msgs],
            2.5,
            after,
        )

    if unrolled:
        after = ()
        for s in range(laps - 2, 0, -1):
            kv_grad, carry = backward(kvs[s], s, carry, after)
            if s == laps - 2:
                lin_out, lin_gate_grad, att_grad, back_msgs = norm(())
            moved = added(kv_grad, hop)
            hop = down(moved, 1)
            after = (moved,)
    else:

        def far_backward(state, given):
            hop, carry = state
            s, kv = given
            kv_grad, carry = backward(kv, s, carry)
            return (down(added(kv_grad, hop), 1), carry), None

        given = (jnp.arange(1, laps - 1), far_kvs)
        (hop, carry), _ = lax.scan(far_backward, (hop, carry), given, reverse=True)
        lin_out, lin_gate_grad, att_grad, back_msgs = norm((carry,))
        after = ()
    joint, pair = pair_states(back_msgs[0], back_msgs[fold - 1], True)
    kv_grad, *query_grads = backward(kv, 0, carry, after)
    joint, far = send_states(joint, True)
    kept, returned = take_states((*pair, *far), True)
    total = added(kv_grad, hop)
    part = jax.ShapeDtypeStruct((tokens, heads * DH), f32)
    lin_query_grad, key_part, value_part = whole_call(
        functools.partial(lin_local_kernel, heads, fold),
        place,
        (log_rows, log_cols, lin_query, lin_key, lin_value, att_grad, *carried),
        [flat, part, part],
        3.4,
    )
    outs, kv_grads = list(outs), [total]
    if fold > 1:
        outs[1], query_grads[1] = swap(outs[1]), swap(query_grads[1])
        kv_grads.append(swap(total[tokens:]))
    thin = jax.ShapeDtypeStruct(soft_key.shape, bf16)
    lin_key_grad, lin_value_grad, soft_out, soft_query_grad, soft_key_grad, soft_value_grad = whole_call(
        functools.partial(final_kernel, heads, fold),
        place,
        (
            *(log_rows, log_cols, lin_key, lin_value, key_part, value_part),
            *(*returned, *outs, *query_grads, *kv_grads),
        ),
        [flat, flat, flat, flat, thin, thin],
        2.0,
    )
    return (
        lin_out,
        lin_query_grad,
        lin_key_grad,
        lin_value_grad,
        lin_gate_grad,
        soft_out,
        soft_query_grad,
        soft_key_grad,
        soft_value_grad,
    )


def solution(mesh):
    spread = P("ctx", "tp")
    return jax.shard_map(
        body,
        mesh=mesh,
        in_specs=(spread, spread, spread, P("tp", "ctx"), P("tp")) + (spread,) * 6,
        out_specs=(spread,) * 9,
        check_vma=False,
    )
```

```python
import functools

import jax
import jax.numpy as jnp
from jax import lax
from jax.experimental import pallas as pl
from jax.experimental.pallas import tpu as pltpu
from jax.sharding import PartitionSpec as P

DH = 128
LOG2E = 1.4426950408889634
LN2 = 0.6931471805599453
negative_fill = -1e30
f32 = jnp.float32
bf16 = jnp.bfloat16
VMEM_BYTES = 24 * 1024 * 1024
FORWARD_CHUNK = 128
FLOPS_PER_MICRO = 2000 * 10**6
BACKWARD_CHUNK = 256

SMEM_SPEC = pl.BlockSpec(memory_space=pltpu.SMEM)
VMEM_SPEC = pl.BlockSpec(memory_space=pltpu.VMEM)
ANY_SPEC = pl.BlockSpec(memory_space=pl.ANY)


def nn(a, b):
    return jnp.dot(a, b, preferred_element_type=f32)


def nt(a, b):
    return lax.dot_general(a, b, (((1,), (1,)), ((), ())), preferred_element_type=f32)


def tn(a, b):
    return lax.dot_general(a, b, (((0,), (0,)), ((), ())), preferred_element_type=f32)


def whole_call(kernel, place, arrays, outs, micros, after=(), aliases={}, scratch=(), out_spec=VMEM_SPEC):
    def ordered(place, *refs):
        kernel(place, *refs[: len(arrays)], *refs[len(arrays) + len(after) :])

    return pl.pallas_call(
        ordered,
        out_shape=outs,
        in_specs=[SMEM_SPEC] + [VMEM_SPEC] * len(arrays) + [ANY_SPEC] * len(after),
        out_specs=[out_spec] * len(outs),
        scratch_shapes=list(scratch),
        input_output_aliases={i + 1: o for i, o in aliases.items()},
        compiler_params=pltpu.CompilerParams(vmem_limit_bytes=VMEM_BYTES),
        cost_estimate=pl.CostEstimate(
            flops=int(micros * FLOPS_PER_MICRO), bytes_accessed=1, transcendentals=0
        ),
    )(place, *arrays, *after)


def split3(x):
    hi = x.astype(bf16)
    rest = x - hi.astype(f32)
    lo = rest.astype(bf16)
    return hi, lo, (rest - lo.astype(f32)).astype(bf16)


def extra_rows(heads):
    return 16 * pl.cdiv(3 * heads, 16)


def pack_logs(rows):
    heads = rows.shape[0]
    pad = extra_rows(heads) - 3 * heads
    parts = [p.astype(f32) for p in split3(rows)]
    if pad:
        parts.append(jnp.zeros((pad, DH), f32))
    return jnp.concatenate(parts, axis=0).astype(bf16)


def read_logs(ref, heads):
    part = ref[heads * DH :, :].astype(f32)
    return part[:heads] + part[heads : 2 * heads] + part[2 * heads : 3 * heads]


def head_rows(h):
    return slice(h * DH, (h + 1) * DH)


def lin_state_kernel(heads, fold, place, log_ref, key_ref, value_ref, msg_ref, row_ref, col_ref):
    rows = key_ref.shape[0]
    y = place[0]
    later = lax.broadcasted_iota(jnp.int32, (rows, rows), 0)
    earlier = lax.broadcasted_iota(jnp.int32, (rows, rows), 1)
    tri = (earlier <= later).astype(f32)
    logs = log_ref[...]
    exact = lax.Precision.HIGHEST
    dims = (((1,), (1,)), ((), ()))
    by_row = lax.dot_general(logs, tri, dims, precision=exact, preferred_element_type=f32)
    by_col = lax.dot_general(tri, logs, dims, precision=exact, preferred_element_type=f32)
    row_ref[...] = by_row
    col_ref[...] = by_col
    totals = by_row[:, rows - 1 : rows]
    tail = jnp.exp(totals - by_row)
    group = heads // fold
    for g in range(fold):
        slot = lax.rem(g + y, fold) if fold > 1 else 0
        for i in range(group):
            h = g * group + i
            key_t = key_ref[:, head_rows(h)].astype(f32).T * tail[h : h + 1, :]
            state = nn(key_t.astype(bf16), value_ref[:, head_rows(h)])
            msg_ref[slot, head_rows(i), :] = state.astype(bf16)
        wide = jnp.broadcast_to(totals[g * group : (g + 1) * group], (group, DH))
        msg_ref[slot, group * DH :, :] = pack_logs(wide)


def lin_pair_kernel(heads, backward, place, own_ref, rec_ref, out_ref):
    y = place[0]
    own_logs, rec_logs = read_logs(own_ref, heads), read_logs(rec_ref, heads)
    out_ref[heads * DH :, :] = pack_logs(own_logs + rec_logs)
    own_far = (y == 1) if backward else (y == 0)
    near_scale = jnp.exp(jnp.where(own_far, rec_logs, own_logs))
    own_scale = jnp.where(own_far, near_scale, 1.0)
    rec_scale = jnp.where(own_far, 1.0, near_scale)
    for i in range(heads):
        own, rec = own_ref[head_rows(i), :].astype(f32), rec_ref[head_rows(i), :].astype(f32)
        joint = own * own_scale[i : i + 1] + rec * rec_scale[i : i + 1]
        out_ref[head_rows(i), :] = joint.astype(bf16)


def lin_combine_kernel(heads, place, own_ref, rec_ref, out_ref):
    own_logs = read_logs(own_ref, heads)
    out_ref[heads * DH :, :] = pack_logs(own_logs + read_logs(rec_ref, heads))
    scale = jnp.exp(own_logs)
    for i in range(heads):
        own, rec = own_ref[head_rows(i), :].astype(f32), rec_ref[head_rows(i), :].astype(f32)
        out_ref[head_rows(i), :] = (own + rec * scale[i : i + 1]).astype(bf16)


def lin_scan_kernel(heads, fold, count, backward, place, own_ref, rec_ref, *rest):
    far, outs = rest[:count], rest[count:]
    y = place[0]
    if fold > 1:
        own_logs, rec_logs = read_logs(own_ref, heads), read_logs(rec_ref, heads)
        own_near = (y == 1) if backward else (y == 0)
        near_scale = jnp.exp(jnp.where(own_near, own_logs, rec_logs))
    far_scales = []
    passed = jnp.zeros((heads, DH), f32)
    for s in range(count):
        far_scales.append(jnp.exp(passed))
        passed = passed + read_logs(far[s], heads)
    for i in range(heads):
        total = jnp.zeros((DH, DH), f32)
        for s in range(count):
            total = total + far_scales[s][i : i + 1] * far[s][head_rows(i), :].astype(f32)
        if fold == 1:
            outs[0][head_rows(i), :] = total.astype(bf16)
            continue
        own, rec = own_ref[head_rows(i), :].astype(f32), rec_ref[head_rows(i), :].astype(f32)
        beyond = jnp.where(own_near, own, rec) + near_scale[i : i + 1] * total
        outs[0][head_rows(i), :] = jnp.where(own_near, total, beyond).astype(bf16)
        outs[1][head_rows(i), :] = jnp.where(own_near, beyond, total).astype(bf16)


def pick_state(refs, h, group, y):
    i = h % group
    if len(refs) == 1:
        return refs[0][head_rows(i), :]
    own, rec = refs[0][head_rows(i), :].astype(f32), refs[1][head_rows(i), :].astype(f32)
    return jnp.where(y == h // group, own, rec).astype(bf16)


def lin_attend_kernel(
    heads, fold, place, row_ref, col_ref, query_ref, key_ref, value_ref, gate_ref, grad_ref, gain_ref, *rest
):
    states, (att_ref, stat_ref) = rest[:fold], rest[fold:]
    rows = query_ref.shape[0]
    y = place[0]
    causal = lax.broadcasted_iota(jnp.int32, (rows, rows), 0) >= lax.broadcasted_iota(
        jnp.int32, (rows, rows), 1
    )
    squares = jnp.zeros((rows, DH), f32)
    crosses = jnp.zeros((rows, DH), f32)
    for h in range(heads):
        query, key, value = (r[:, head_rows(h)] for r in (query_ref, key_ref, value_ref))
        col = col_ref[:, h : h + 1]
        decay = jnp.exp(jnp.where(causal, col - row_ref[h : h + 1, :], negative_fill))
        weights = (nt(query, key) * decay).astype(bf16)
        state = pick_state(states, h, heads // fold, y)
        att = nn(weights, value) + jnp.exp(col) * nn(query, state)
        att_ref[:, head_rows(h)] = att
        sig = jax.nn.sigmoid(gate_ref[:, head_rows(h)].astype(f32))
        scaled = grad_ref[:, head_rows(h)].astype(f32) * gain_ref[:, head_rows(h)] * sig
        squares = squares + att * att
        crosses = crosses + scaled * att
    stat_ref[...] = jnp.concatenate(
        (
            jnp.sum(squares.T, axis=0, keepdims=True),
            jnp.sum(crosses.T, axis=0, keepdims=True),
            jnp.zeros((6, rows), f32),
        ),
        axis=0,
    )


def lin_norm_kernel(
    heads, fold, width, place, row_ref, att_ref, gate_ref, grad_ref, gain_ref, query_ref, own_ref, oth_ref, *rest
):
    *stat_refs, out_ref, gate_grad_ref, att_grad_ref, msg_ref = rest
    y = place[0]
    rows = query_ref.shape[0]
    stats = sum((r[...] for r in stat_refs[1:]), stat_refs[0][...])
    stats = jnp.concatenate((stats, jnp.zeros((DH - 8, rows), f32)), axis=0).T
    scaling = lax.rsqrt(stats[:, 0:1] / width + 1e-05)
    cross = scaling * stats[:, 1:2] / width
    group = heads // fold
    lead = jnp.exp(row_ref[...])
    for g in range(fold):
        slot = lax.rem(g + y, fold) if fold > 1 else 0
        for i in range(group):
            h = g * group + i
            gain = gain_ref[:, head_rows(h)]
            sig = jax.nn.sigmoid(gate_ref[:, head_rows(h)].astype(f32))
            normed = att_ref[:, head_rows(h)] * scaling
            scaled = grad_ref[:, head_rows(h)].astype(f32) * gain * sig
            out_ref[:, head_rows(h)] = (normed * gain * sig).astype(bf16)
            gate_grad_ref[:, head_rows(h)] = (scaled * normed * (1.0 - sig)).astype(bf16)
            att_grad = (scaling * (scaled - normed * cross)).astype(bf16)
            att_grad_ref[:, head_rows(h)] = att_grad
            query_t = query_ref[:, head_rows(h)].astype(f32).T * lead[h : h + 1, :]
            msg_ref[slot, head_rows(i), :] = nn(query_t.astype(bf16), att_grad).astype(bf16)
    msg_ref[0, group * DH :, :] = own_ref[group * DH :, :]
    if fold > 1:
        msg_ref[1, group * DH :, :] = oth_ref[group * DH :, :]


def lin_local_kernel(heads, fold, place, row_ref, col_ref, query_ref, key_ref, value_ref, att_grad_ref, *rest):
    states, (query_grad_ref, key_part_ref, value_part_ref) = rest[:fold], rest[fold:]
    y = place[0]
    rows = query_ref.shape[0]
    first = lax.broadcasted_iota(jnp.int32, (rows, rows), 0)
    second = lax.broadcasted_iota(jnp.int32, (rows, rows), 1)
    causal, causal_t = first >= second, first <= second
    for h in range(heads):
        query, key, value, grad = (
            r[:, head_rows(h)] for r in (query_ref, key_ref, value_ref, att_grad_ref)
        )
        col, row = col_ref[:, h : h + 1], row_ref[h : h + 1, :]
        decay = jnp.exp(jnp.where(causal, col - row, negative_fill))
        decay_t = jnp.exp(jnp.where(causal_t, row - col, negative_fill))
        state = pick_state(states, h, heads // fold, y)
        grad_weights = (nt(grad, value) * decay).astype(bf16)
        grad_weights_t = (nt(value, grad) * decay_t).astype(bf16)
        weights_t = (nt(key, query) * decay_t).astype(bf16)
        query_grad = nn(grad_weights, key) + jnp.exp(col) * nt(grad, state)
        query_grad_ref[:, head_rows(h)] = query_grad.astype(bf16)
        key_part_ref[:, head_rows(h)] = nn(grad_weights_t, query)
        value_part_ref[:, head_rows(h)] = nn(weights_t, grad)


def final_kernel(heads, fold, place, row_ref, col_ref, key_ref, value_ref, key_part_ref, value_part_ref, *rest):
    states, rest = rest[:fold], rest[fold:]
    *halves, key_made, value_made, sems = rest
    halves, outs = halves[:-6], halves[-6:]
    y = place[0]
    rows = key_ref.shape[0]
    copies = []

    def send(source, target):
        copies.append(pltpu.make_async_copy(source, target, sems.at[len(copies)]))
        copies[-1].start()

    for i in range(fold):
        at = (y + i) % fold
        for out, part in ((outs[2], halves[i]), (outs[3], halves[fold + i])):
            size = part.shape[1]
            send(part, out.at[:, pl.ds(pl.multiple_of(at * size, DH), size)])
        for j in range(2):
            part = halves[2 * fold + i].at[:rows, j * DH : (j + 1) * DH]
            send(part, outs[4 + j].at[:, pl.ds(pl.multiple_of(at * DH, DH), DH)])
    for h in range(heads):
        span = head_rows(h)
        key, value = key_ref[:, span], value_ref[:, span]
        tail = jnp.exp(row_ref[h : h + 1, rows - 1 : rows] - col_ref[:, h : h + 1])
        state = pick_state(states, h, heads // fold, y)
        key_made[:, span] = (key_part_ref[:, span] + tail * nt(value, state)).astype(bf16)
        value_made[:, span] = (value_part_ref[:, span] + tail * nn(key, state)).astype(bf16)
        if h % 2 == 1:
            pair = slice((h - 1) * DH, (h + 1) * DH)
            send(key_made.at[:, pair], outs[0].at[:, pair])
            send(value_made.at[:, pair], outs[1].at[:, pair])
    for copy in copies:
        copy.wait()


def diagonal_mask(y, keys, first, count, tokens, rows):
    key_at = lax.rem(lax.broadcasted_iota(jnp.int32, (keys, count), 0) + y * tokens, rows)
    query_at = lax.rem(lax.broadcasted_iota(jnp.int32, (keys, count), 1) + first + y * tokens, rows)
    return key_at <= query_at


def soft_pack_kernel(place, rows_ref, out_ref):
    half = rows_ref.shape[1] // 2
    out_ref[...] = rows_ref[:, pl.ds(pl.multiple_of((1 - place[0]) * half, DH), half)]


def head_of_rows(y, group, h, own_ref, rec_ref):
    if rec_ref is None:
        return own_ref[:, head_rows(h)]
    own = own_ref[:, pl.ds(pl.multiple_of((y * group + h) * DH, DH), DH)]
    return jnp.concatenate((own, rec_ref[:, head_rows(h)]), axis=0)


def soft_forward_kernel(fold, tokens, group, diagonal, last, place, *refs):
    refs = list(refs)
    take = lambda count: [refs.pop(0) for _ in range(count)]
    query_ref = take(1)[0]
    kv_refs = take(fold)
    grad_ref = take(1)[0] if last else None
    query_rec = take(1)[0] if fold > 1 else None
    grad_rec = take(1)[0] if fold > 1 and last else None
    old_peak, old_total, old_acc = take(3) if not diagonal else (None,) * 3
    outs = take(fold + 2 if last else 3)
    peak, total, acc = refs if last else outs
    y = place[0]
    rows = tokens * fold

    def compute():
        kv = jnp.concatenate([r[...] for r in kv_refs], axis=0)
        key, value = kv[:, :DH], kv[:, DH:]
        step = min(FORWARD_CHUNK, rows)
        for h in range(group):
            query = head_of_rows(y, group, h, query_ref, query_rec)
            for at in range(0, rows, step):
                span = slice(at, at + step)
                scores = nt(key, query[span]) * (LOG2E * DH**-0.5)
                if diagonal:
                    mask = diagonal_mask(y, rows, at, step, tokens, rows)
                    scores = jnp.where(mask, scores, negative_fill)
                    fresh = jnp.max(scores, axis=0, keepdims=True)
                    probs = jnp.exp2(scores - fresh)
                    total[h, :, span] = jnp.sum(probs, axis=0, keepdims=True)
                    acc[h, :, span] = tn(value, probs.astype(bf16))
                else:
                    old = old_peak[h, :, span]
                    fresh = jnp.maximum(old, jnp.max(scores, axis=0, keepdims=True))
                    probs = jnp.exp2(scores - fresh)
                    fade = jnp.exp2(old - fresh)
                    total[h, :, span] = old_total[h, :, span] * fade + jnp.sum(
                        probs, axis=0, keepdims=True
                    )
                    acc[h, :, span] = old_acc[h, :, span] * fade + tn(value, probs.astype(bf16))
                peak[h, :, span] = fresh

    if diagonal:
        compute()
    else:
        reached = place[1] >= place[2]
        pl.when(reached)(compute)
        if last:

            @pl.when(jnp.logical_not(reached))
            def _():
                peak[...], total[...], acc[...] = old_peak[...], old_total[...], old_acc[...]

    if last:
        for h in range(group):
            out_t = (acc[h] / total[h]).astype(bf16).astype(f32)
            out = out_t.T.astype(bf16)
            for i in range(fold):
                outs[i][:, head_rows(h)] = out[i * tokens : (i + 1) * tokens]
            grad_t = head_of_rows(y, group, h, grad_ref, grad_rec).astype(f32).T
            outs[fold][h] = peak[h] + jnp.log(total[h]) * LOG2E
            outs[fold + 1][h] = jnp.sum(grad_t * out_t, axis=0, keepdims=True)


def soft_forward(place, query, grad, rec, kv, carry, last, after=()):
    tokens, fold = query.shape[0], len(kv)
    rows, group = tokens * fold, query.shape[1] // DH // fold
    diagonal = carry is None
    lines = jax.ShapeDtypeStruct((group, 1, rows), f32)
    talls = jax.ShapeDtypeStruct((group, DH, rows), f32)
    own = (query, *kv, grad) if last else (query, *kv)
    arrays = (*own, *(rec if last else rec[:1]), *(() if diagonal else carry))
    aliases, scratch = {}, ()
    if last:
        outs = [jax.ShapeDtypeStruct((tokens, group * DH), bf16)] * fold + [lines, lines]
        scratch = [pltpu.VMEM(a.shape, f32) for a in (lines, lines, talls)]
    else:
        outs = [lines, lines, talls]
        if not diagonal:
            aliases = {len(arrays) - 3 + i: i for i in range(3)}
    kernel = functools.partial(soft_forward_kernel, fold, tokens, group, diagonal, last)
    return whole_call(kernel, place, arrays, outs, 3.0 if last else 2.6, after, aliases, scratch)


def soft_backward_kernel(fold, tokens, group, diagonal, first, place, *refs):
    refs = list(refs)
    take = lambda count: [refs.pop(0) for _ in range(count)]
    query_ref, grad_ref, log_ref, delta_ref = take(4)
    kv_refs = take(fold)
    query_rec, grad_rec = take(2) if fold > 1 else (None, None)
    old_acc = take(1)[0] if not first else None
    kv_grad_ref, *outs = refs
    y = place[0]
    rows = tokens * fold

    def compute():
        kv = jnp.concatenate([r[...] for r in kv_refs], axis=0)
        key, value = kv[:, :DH], kv[:, DH:]
        step = min(BACKWARD_CHUNK, rows)
        key_acc, value_acc = jnp.zeros((rows, DH), f32), jnp.zeros((rows, DH), f32)
        for h in range(group):
            query = head_of_rows(y, group, h, query_ref, query_rec)
            grad = head_of_rows(y, group, h, grad_ref, grad_rec)
            for at in range(0, rows, step):
                span = slice(at, at + step)
                scores = nt(key, query[span]) * (LOG2E * DH**-0.5) - log_ref[h, :, span]
                if diagonal:
                    mask = diagonal_mask(y, rows, at, step, tokens, rows)
                    scores = jnp.where(mask, scores, negative_fill)
                probs = jnp.exp2(scores)
                score_grad = (probs * (nt(value, grad[span]) - delta_ref[h, :, span])).astype(bf16)
                value_acc += nn(probs.astype(bf16), grad[span])
                key_acc += nn(score_grad, query[span])
                query_grad = tn(key, score_grad)
                if not first:
                    query_grad += old_acc[h, :, span]
                if diagonal:
                    query_grad = (query_grad * DH**-0.5).T.astype(bf16)
                    i, begin = at // tokens, at % tokens
                    outs[i][begin : begin + step, head_rows(h)] = query_grad
                else:
                    outs[0][h, :, span] = query_grad
        kv_grad_ref[:, :DH] = key_acc * DH**-0.5
        kv_grad_ref[:, DH:] = value_acc

    if diagonal:
        compute()
        return
    reached = place[1] >= place[2]
    pl.when(reached)(compute)

    @pl.when(jnp.logical_not(reached))
    def _():
        kv_grad_ref[...] = jnp.zeros_like(kv_grad_ref)
        if first:
            outs[0][...] = jnp.zeros_like(outs[0])


def soft_backward(place, query, grad, rec, logs, deltas, kv, carry, diagonal, after=()):
    tokens, fold = query.shape[0], len(kv)
    rows, group = tokens * fold, query.shape[1] // DH // fold
    first = carry is None
    arrays = (query, grad, logs, deltas, *kv, *rec, *(() if first else (carry,)))
    outs = [jax.ShapeDtypeStruct((rows, 2 * DH), f32)]
    aliases = {}
    if diagonal:
        outs += [jax.ShapeDtypeStruct((tokens, group * DH), bf16)] * fold
    else:
        outs += [jax.ShapeDtypeStruct((group, DH, rows), f32)]
        if not first:
            aliases = {len(arrays) - 1: 1}
    kernel = functools.partial(soft_backward_kernel, fold, tokens, group, diagonal, first)
    return whole_call(kernel, place, arrays, outs, 0.01 if diagonal else 3.4, after, aliases)


def body(
    lin_query,
    lin_key,
    lin_value,
    log_decay,
    norm_gain,
    lin_gate,
    lin_grad,
    soft_query,
    soft_key,
    soft_value,
    soft_grad,
):
    count = lax.axis_size("ctx")
    kv_heads = soft_key.shape[1] // DH
    fold = 2 if kv_heads == 2 and count % 2 == 0 else 1
    laps = count // fold
    index = lax.axis_index("ctx")
    y, z = lax.rem(index, fold), lax.div(index, fold)
    place = jnp.stack((y, z)).astype(jnp.int32)
    tokens = soft_query.shape[0]
    rows = tokens * fold
    heads = lin_query.shape[1] // DH
    group = heads // fold
    width = lin_query.shape[1] * lax.axis_size("tp")
    gain = norm_gain[None, :]

    def swap(a):
        return lax.ppermute(a, "ctx", [(i, i ^ 1) for i in range(count)])

    def up(a, s, least=0):
        pairs = [(i, i + fold * s) for i in range(fold * least, count - fold * s)]
        return lax.ppermute(a, "ctx", pairs)

    def down(a, s, least=0):
        pairs = [(i + fold * s, i) for i in range(fold * max(least - s, 0), count - fold * s)]
        return lax.ppermute(a, "ctx", pairs)

    def own_columns(a):
        size = a.shape[1] // 2
        return a if fold == 1 else jnp.where(y == 0, a[:, :size], a[:, size:])

    def partner_columns(a):
        size = a.shape[1] // 2
        return jnp.where(y == 0, a[:, size:], a[:, :size])

    def each(move, parts, *way):
        return [move(a, *way) for a in parts]

    def at_lap(s):
        return jnp.concatenate((place, jnp.asarray(s, jnp.int32)[None]))

    early = ()
    kv = [jnp.concatenate((own_columns(soft_key), own_columns(soft_value)), axis=1)]
    if fold > 1:
        kv_sent = jnp.concatenate((partner_columns(soft_key), partner_columns(soft_value)), axis=1)
        kv.append(swap(kv_sent))
        early = (kv_sent, kv[0])

    msg_rows = group * DH + extra_rows(group)
    msg = jax.ShapeDtypeStruct((msg_rows, DH), bf16)
    msgs = jax.ShapeDtypeStruct((fold, msg_rows, DH), bf16)
    state = jax.ShapeDtypeStruct((group * DH, DH), bf16)
    flat = jax.ShapeDtypeStruct((tokens, heads * DH), bf16)
    state_msgs, log_rows, log_cols = whole_call(
        functools.partial(lin_state_kernel, heads, fold),
        place,
        (log_decay, lin_key, lin_value),
        [
            msgs,
            jax.ShapeDtypeStruct((heads, tokens), f32),
            jax.ShapeDtypeStruct((tokens, heads), f32),
        ],
        1.4,
        early,
    )
    own_msg, oth_msg = state_msgs[0], state_msgs[fold - 1]
    rec = ()
    if fold > 1:
        half = jax.ShapeDtypeStruct((tokens, group * DH), bf16)
        (sent,) = whole_call(soft_pack_kernel, place, (soft_query,), [half], 0.6, (state_msgs,))
        rec = (swap(sent),)
    unrolled = laps <= 8
    if unrolled:
        kvs = [kv]
        for s in range(1, laps):
            kvs.append(each(up, kvs[-1], 1, s - 1))

    def pair_states(own, other, backward, after=()):
        if fold == 1:
            return own, (own, own)
        rec = swap(other)
        kernel = functools.partial(lin_pair_kernel, group, backward)
        return whole_call(kernel, place, (own, rec), [msg], 0.6, after)[0], (own, rec)

    def send_states(joint, backward, after=()):
        got, step, move = [], 1, down if backward else up
        while step < laps:
            got.append(move(joint, step))
            step *= 2
            if step < laps:
                kernel = functools.partial(lin_combine_kernel, group)
                (joint,) = whole_call(kernel, place, (joint, got[-1]), [msg], 0.6, after)
        return joint, got

    def take_states(sent, backward, after=()):
        got = whole_call(
            functools.partial(lin_scan_kernel, group, fold, len(sent) - 2, backward),
            place,
            sent,
            [state] * fold,
            0.7,
            after=after,
        )
        return got[0], ((got[0], swap(got[1])) if fold > 1 else tuple(got))

    def forward(kv, s, carry, last, after=()):
        return soft_forward(at_lap(s), soft_query, soft_grad, rec, kv, carry, last, after)

    def backward(kv, s, carry, after=()):
        whole = (soft_query, soft_grad, rec, logs, deltas, kv, carry)
        return soft_backward(at_lap(s), *whole, isinstance(s, int) and s == 0, after)

    joint, pair = pair_states(own_msg, oth_msg, False)
    if fold > 1:
        (grad_sent,) = whole_call(soft_pack_kernel, place, (soft_grad,), [half], 0.6, (joint,))
        rec += (swap(grad_sent),)
    joint, far = send_states(joint, False)
    soft = forward(kv, 0, None, False, (joint,))
    if unrolled:
        for s in range(1, laps - 1):
            soft = forward(kvs[s], s, soft, False)
        last_kv = kvs[-1]
    else:

        def far_forward(state, s):
            kv, soft = state
            kv = each(up, kv, 1)
            return (kv, forward(kv, s, soft, False)), kv

        (last_kv, soft), far_kvs = lax.scan(far_forward, (kv, soft), jnp.arange(1, laps - 1))
        last_kv = each(up, last_kv, 1)
    kept, carried = take_states((*pair, *far), False, (soft[0],))
    soft = forward(last_kv, laps - 1, soft, True, (kept,))
    outs, (logs, deltas) = list(soft[:fold]), soft[fold:]
    if fold > 1:
        outs[1] = swap(outs[1])
    attended, stats = whole_call(
        functools.partial(lin_attend_kernel, heads, fold),
        place,
        (log_rows, log_cols, lin_query, lin_key, lin_value, lin_gate, lin_grad, gain, *carried),
        [
            jax.ShapeDtypeStruct((tokens, heads * DH), f32),
            jax.ShapeDtypeStruct((8, tokens), f32),
        ],
        2.0,
        (logs,),
    )
    tp = lax.axis_size("tp")
    if tp <= 4 and tp & (tp - 1) == 0:
        all_stats = [stats] + [
            lax.ppermute(stats, "tp", [(i, i ^ k) for i in range(tp)]) for k in range(1, tp)
        ]
    else:
        all_stats = [lax.psum(stats, "tp")]

    def added(kv_grad, hop):
        return (kv_grad + hop.astype(f32)).astype(bf16)

    kv_grad, carry = backward(last_kv, laps - 1, None, (stats, outs[-1]))
    hop = down(kv_grad.astype(bf16), 1, laps - 1 if unrolled else 0)

    def norm(after):
        return whole_call(
            functools.partial(lin_norm_kernel, heads, fold, width),
            place,
            (log_rows, attended, lin_gate, lin_grad, gain, lin_query, own_msg, oth_msg, *all_stats),
            [flat, flat, flat, msgs],
            2.5,
            after,
        )

    lin_out, lin_gate_grad, att_grad, back_msgs = norm((carry,))
    if unrolled:
        after = (back_msgs,)
        for s in range(laps - 2, 0, -1):
            kv_grad, carry = backward(kvs[s], s, carry, after)
            moved = added(kv_grad, hop)
            hop = down(moved, 1, s)
            if s == laps - 2:
                joint, pair = pair_states(back_msgs[0], back_msgs[fold - 1], True, (moved,))
            after = (joint, moved)
    else:
        after = ()

        def far_backward(state, given):
            hop, carry = state
            s, kv = given
            kv_grad, carry = backward(kv, s, carry)
            return (down(added(kv_grad, hop), 1), carry), None

        given = (jnp.arange(1, laps - 1), far_kvs)
        (hop, carry), _ = lax.scan(far_backward, (hop, carry), given, reverse=True)
        joint, pair = pair_states(back_msgs[0], back_msgs[fold - 1], True)
    joint, far = send_states(joint, True, after)
    kv_grad, *query_grads = backward(kv, 0, carry, (joint,))
    kept, returned = take_states((*pair, *far), True)
    total = added(kv_grad, hop)
    part = jax.ShapeDtypeStruct((tokens, heads * DH), f32)
    lin_query_grad, key_part, value_part = whole_call(
        functools.partial(lin_local_kernel, heads, fold),
        place,
        (log_rows, log_cols, lin_query, lin_key, lin_value, att_grad, *carried),
        [flat, part, part],
        0.01,
    )
    kv_grads = [total]
    if fold > 1:
        query_grads[1] = swap(query_grads[1])
        kv_grads.append(swap(total[tokens:]))
    thin = jax.ShapeDtypeStruct(soft_key.shape, bf16)
    lin_key_grad, lin_value_grad, soft_out, soft_query_grad, soft_key_grad, soft_value_grad = whole_call(
        functools.partial(final_kernel, heads, fold),
        place,
        (
            *(log_rows, log_cols, lin_key, lin_value, key_part, value_part),
            *(*returned, *outs, *query_grads, *kv_grads),
        ),
        [flat, flat, flat, flat, thin, thin],
        2.0,
        scratch=(
            pltpu.VMEM(flat.shape, bf16),
            pltpu.VMEM(flat.shape, bf16),
            pltpu.SemaphoreType.DMA((4 * fold + heads,)),
        ),
        out_spec=ANY_SPEC,
    )
    return (
        lin_out,
        lin_query_grad,
        lin_key_grad,
        lin_value_grad,
        lin_gate_grad,
        soft_out,
        soft_query_grad,
        soft_key_grad,
        soft_value_grad,
    )


def solution(mesh):
    spread = P("ctx", "tp")
    return jax.shard_map(
        body,
        mesh=mesh,
        in_specs=(spread, spread, spread, P("tp", "ctx"), P("tp")) + (spread,) * 6,
        out_specs=(spread,) * 9,
        check_vma=False,
    )
```
